32 devices in a mesh: group: 2 (over y), tile: 4 (over z), strip: 2 (over x), mode: 2 (over core).
Axes of the slice: x: 2, y: 2, z: 4, core: 2. Of those that a mesh axis runs over, the one named last changes fastest.
Arguments:
- object_field: bfloat16 [4, 2, 256, 2048], P('group', 'mode', 'strip', 'tile'), parts along dimension 0, may hold values from -4 to 4
- probe_modes: float32 [4, 2, 128, 128], P('group'), parts along dimension 0, may hold values from -5 to 5
- measured: float32 [4, 32, 128, 128], P(('group', 'strip'), ('tile', 'mode')), parts along dimension 0, may hold values from 0.25 to 16
- pos_tile: int32 [4, 32, 1], P(('group', 'strip')), parts along dimension 0, may hold values from 0 to 3; in each aligned block of 4 rows (0 to 3, 4 to 7, ..., all dimensions but the last counted through in order) at most 2 rows name the same one
- off_row: int32 [4, 32], P(('group', 'strip')), parts along dimension 0, may hold values from 0 to 128, as said below
- off_col: int32 [4, 32], P(('group', 'strip')), parts along dimension 0, may hold values from 0 to 512, as said below
Outputs:
- object_grad: float32 [4, 2, 256, 2048], P('group', 'mode', 'strip', 'tile'), parts along dimension 0
- probe_grad: float32 [4, 2, 128, 128], P('group'), parts along dimension 0
The draws below stay inside these ranges and needn't reach their ends.
There are 2 independent parts, one for each index of `group`. The reference program is written for one: setup_inputs(seed, part) draws one part's arguments, and reference() takes and returns one part's arrays. A program takes and returns all parts, laid end to end along the dimension named above; each array names one. Nothing has to cross between parts.
Inputs may be any that keep to these rules, and one draw needn't show every extreme that they name: `pos_tile`: blocks of 4 consecutive positions belong to one device; within such a block at most 2 positions name the same tile, and in every draw some block has exactly 2 on one tile. `off_row`: each row offset is below 64 or above 64. `off_col`: each column offset is below 64 or above 448.
All inputs are finite; a program needn't handle non-finite values.
Results may differ from the reference program's by a relative error of at most 0.02.
The reference program's roundings to bfloat16 on the way count: a program that leaves them out, or rounds other values in their place, can miss the bound.
Values may be sent and summed in bfloat16 or wider, within the bound.
A program may use at most 64 MiB of HBM per device.

```python
import math
import jax
import jax.numpy as jnp
import numpy as np
from jax import lax

PAT = 128
MODES = 2
SLICES = 2
TH = 128
POS_DEV = 4
TW = 512
CAP = 2
STRIP_POS = 32
OH = 256
OW = 2048
N_TILE = 4
N_STRIP = 2


def edge_offsets(key, span):
    key_low, key_high, key_pick = jax.random.split(key, 3)
    shape = (N_STRIP, STRIP_POS)
    low_part = jax.random.randint(key_low, shape, 0, PAT // 2)
    high_part = jax.random.randint(key_high, shape, span + 1 - PAT // 2, span + 1)
    picker = jax.random.randint(key_pick, shape, 0, 2)
    return jnp.where(picker == 1, high_part, low_part).astype(jnp.int32)


def draw_off_row(key, part):
    key = jax.random.fold_in(key, 11)
    return edge_offsets(key, TH)


def draw_off_col(key, part):
    key = jax.random.fold_in(key, 12)
    return edge_offsets(key, TW)


def shard_levels(key, extent, cuts, least, high):
    loudness = 1.0
    for position, blocks in cuts:
        draws = jax.random.uniform(jax.random.fold_in(jax.random.fold_in(key, 6), position), (blocks,), jnp.float32, least / len(cuts), high / len(cuts))
        loudness = loudness * jnp.repeat(jnp.exp(draws), extent[position] // blocks).reshape((-1,) + (1,) * (len(extent) - 1 - position))
    return loudness


def deal_out(rng, own, number, rows, number_of, top, limit, slope):
    order = jax.random.permutation(rng, number_of)
    crowded, usual = shares(number_of, rows * top, limit, slope, True), shares(number_of, rows * top, limit, slope, False)
    places = jnp.arange(number_of)

    def named(tallies, offset_by):
        used = int((tallies > 0).sum())
        fixed = max(1, used // 4)
        moved = fixed + (places - fixed + offset_by * (used - fixed)) % max(1, number_of - fixed)
        return jnp.zeros((number_of,), jnp.int32).at[order[jnp.where(places < fixed, places, moved)]].set(jnp.asarray(tallies, jnp.int32))

    tallies = jnp.where(number % 4 == 0, named(crowded, number // 4), named(usual, number - number // 4 - 1))
    mixed = jax.random.permutation(jax.random.fold_in(own, 3), number_of)
    donor, sink = mixed[0:number_of // 2 * 2:2], mixed[1:number_of // 2 * 2:2]
    room = jnp.minimum(tallies[donor] - 1, limit - tallies[sink]) // 2
    room = jnp.where((donor == order[0]) | (sink == order[0]) | (tallies[sink] == 0), 0, jnp.maximum(room, 0))
    moved = jax.random.randint(jax.random.fold_in(own, 4), (number_of // 2,), 0, 1 << 20) % (room + 1)
    tallies = tallies.at[donor].add(-moved).at[sink].add(moved)
    members = jnp.searchsorted(jnp.cumsum(tallies), jnp.arange(rows * top), side="right").astype(jnp.int32)
    grid = members.reshape(top, rows).T
    grid = grid[jax.random.permutation(jax.random.fold_in(own, 1), rows)]
    offset_by = jax.random.randint(jax.random.fold_in(own, 2), (rows, 1), 0, top)
    return jnp.take_along_axis(grid, (jnp.arange(top)[None, :] + offset_by) % top, axis=1)


def shares(number_of, total, bound, lean, full):
    loads = [(1 << 20) // math.isqrt(grade ** lean) + 1 for grade in range(1, number_of + 1)]
    largest = bound if full else min(bound, max(-(-total // number_of), total * loads[0] // sum(loads)))
    least = 1 if total - largest >= number_of - 1 else 0
    holding, surplus = [largest] + [least] * (number_of - 1), total - largest - least * (number_of - 1)
    while surplus > 0:
        movable = [i for i in range(1, number_of) if holding[i] < largest] or [i for i in range(1, number_of) if holding[i] < bound]
        mass, left = sum([loads[i] for i in movable]), surplus
        for i in movable:
            more = min(bound - holding[i], max(1, left * loads[i] // mass), surplus)
            holding[i] = holding[i] + more
            surplus = surplus - more
    return np.array(holding)


def noise(rng, dims, scale, limit, cuts=(), held_as=jnp.bfloat16):
    drawn = scale * jax.random.normal(rng, dims, jnp.float32)
    if cuts:
        drawn = drawn * shard_levels(rng, dims, cuts, -0.22, 0.18)
    return jnp.clip(drawn, -limit, limit).astype(held_as)


def setup_inputs(seed: int = 0, part: int = 0) -> dict:
    key_list = jax.random.split(jax.random.key(seed), 7)
    part_keys = jax.random.split(jax.random.fold_in(key_list[6], part), 7)
    object_field = noise(part_keys[0], (2, SLICES, OH, OW), 0.7, 4.0, ((1, 2), (2, 2), (3, 4)))
    probe_modes = noise(part_keys[1], (2, MODES, PAT, PAT), 0.7, 5.0, (), jnp.float32)
    measured = jnp.clip(jnp.exp(math.log(16.0) - 4.158883 * jax.random.uniform(part_keys[2], (N_STRIP, STRIP_POS, PAT, PAT), jnp.float32) ** shard_levels(part_keys[2], (N_STRIP, STRIP_POS, PAT, PAT), ((0, 2), (1, 8)), -0.2, 0.2)), 0.25, 16.0)
    pos_tile_keys = jax.random.split(jax.random.fold_in(part_keys[3], 1), N_STRIP * STRIP_POS // POS_DEV)
    pos_tile_turns = jax.random.permutation(jax.random.fold_in(part_keys[3], 3), N_STRIP * STRIP_POS // POS_DEV)
    pos_tile = jax.vmap(lambda own, number: deal_out(jax.random.fold_in(part_keys[3], 2), own, number, POS_DEV, N_TILE, 1, CAP, 2))(pos_tile_keys, pos_tile_turns).reshape((N_STRIP, STRIP_POS, 1))
    off_row = draw_off_row(jax.random.fold_in(jax.random.fold_in(key_list[6], part), 71), part)
    off_col = draw_off_col(jax.random.fold_in(jax.random.fold_in(key_list[6], part), 71), part)
    return dict(object_field=object_field, probe_modes=probe_modes, measured=measured, pos_tile=pos_tile, off_row=off_row, off_col=off_col)


prop_phase = 60.0

def to_half(values):
    return lax.optimization_barrier(values.astype(jnp.bfloat16)).astype(jnp.float32)

def dft_tables(length):
    indices = jnp.arange(length, dtype=jnp.int32)
    products = indices[:, None] * indices[None, :] % length
    angles = products.astype(jnp.float32) * (2.0 * jnp.pi / length)
    scale_factor = 1.0 / jnp.sqrt(jnp.float32(length))
    return (to_half(jnp.cos(angles) * scale_factor), to_half(-jnp.sin(angles) * scale_factor))

def propagator(length):
    indices = jnp.arange(length, dtype=jnp.int32)
    shifted = (indices + length // 2) % length - length // 2
    frequency = shifted.astype(jnp.float32) / length
    phases = -prop_phase * (frequency[:, None] ** 2 + frequency[None, :] ** 2)
    return (jnp.cos(phases), jnp.sin(phases))

def make_tables(length):
    cos_table, sin_table = dft_tables(length)
    prop_cos, prop_sin = propagator(length)
    return (cos_table, sin_table, -sin_table, prop_cos, prop_sin)

def right_mult(left, table):
    return jnp.einsum('nij,jk->nik', left, table, precision=lax.Precision.HIGHEST)

def left_mult(table, right):
    return jnp.einsum('ij,njk->nik', table, right, precision=lax.Precision.HIGHEST)

def transform(field_re, field_im, cos_table, sin_table):
    half_re = to_half(field_re)
    half_im = to_half(field_im)
    mid_re = to_half(right_mult(half_re, cos_table) - right_mult(half_im, sin_table))
    mid_im = to_half(right_mult(half_re, sin_table) + right_mult(half_im, cos_table))
    out_re = left_mult(cos_table, mid_re) - left_mult(sin_table, mid_im)
    out_im = left_mult(sin_table, mid_re) + left_mult(cos_table, mid_im)
    return (out_re, out_im)

def position_terms(window, probe_re, probe_im, observed, tables):
    cos_table, sin_table, conj_table, prop_cos, prop_sin = tables
    front_re, front_im = (window[0, 0], window[0, 1])
    rear_re, rear_im = (window[1, 0], window[1, 1])
    wave_a_re = probe_re * front_re - probe_im * front_im
    wave_a_im = probe_re * front_im + probe_im * front_re
    spec_re, spec_im = transform(wave_a_re, wave_a_im, cos_table, sin_table)
    kick_re = spec_re * prop_cos - spec_im * prop_sin
    kick_im = spec_re * prop_sin + spec_im * prop_cos
    inner_re, inner_im = transform(kick_re, kick_im, cos_table, conj_table)
    wave_b_re = inner_re * rear_re - inner_im * rear_im
    wave_b_im = inner_re * rear_im + inner_im * rear_re
    far_re, far_im = transform(wave_b_re, wave_b_im, cos_table, sin_table)
    intensity = lax.optimization_barrier(jnp.sum(far_re * far_re + far_im * far_im, axis=0))
    amp_factor = 1.0 - jnp.sqrt(observed) / jnp.sqrt(intensity + 1.0)
    back_b_re, back_b_im = transform(far_re * amp_factor, far_im * amp_factor, cos_table, conj_table)
    grad_in_re = rear_re * back_b_re + rear_im * back_b_im
    grad_in_im = rear_re * back_b_im - rear_im * back_b_re
    back_spec_re, back_spec_im = transform(grad_in_re, grad_in_im, cos_table, sin_table)
    spec_h_re = back_spec_re * prop_cos + back_spec_im * prop_sin
    spec_h_im = back_spec_im * prop_cos - back_spec_re * prop_sin
    back_a_re, back_a_im = transform(spec_h_re, spec_h_im, cos_table, conj_table)
    grad_a_re = lax.optimization_barrier(jnp.sum(probe_re * back_a_re + probe_im * back_a_im, axis=0))
    grad_a_im = lax.optimization_barrier(jnp.sum(probe_re * back_a_im - probe_im * back_a_re, axis=0))
    grad_b_re = lax.optimization_barrier(jnp.sum(inner_re * back_b_re + inner_im * back_b_im, axis=0))
    grad_b_im = lax.optimization_barrier(jnp.sum(inner_re * back_b_im - inner_im * back_b_re, axis=0))
    pterm_re = front_re * back_a_re + front_im * back_a_im
    pterm_im = front_re * back_a_im - front_im * back_a_re
    gradient_window = jnp.stack([jnp.stack([grad_a_re, grad_a_im]), jnp.stack([grad_b_re, grad_b_im])]).astype(jnp.bfloat16)
    return (gradient_window, jnp.stack([pterm_re, pterm_im]))

def reference(object_field, probe_modes, measured, pos_tile, off_row, off_col):
    length = PAT
    margin = PAT // 2
    padded = jnp.pad(object_field, ((0, 0), (0, 0), (margin, margin), (margin, margin)))
    tables = make_tables(length)
    strip_ids = jnp.repeat(jnp.arange(N_STRIP, dtype=jnp.int32), STRIP_POS)
    row_starts = (strip_ids * TH + off_row.reshape(-1)).astype(jnp.int32)
    col_starts = (pos_tile.reshape(-1) * TW + off_col.reshape(-1)).astype(jnp.int32)
    observed_all = measured.reshape(-1, length, length)
    zero_index = jnp.zeros((), jnp.int32)

    def advance(carry, inputs):
        grad_grid, running = carry
        row_at, col_at, observed = inputs
        row_at = row_at.astype(jnp.int32)
        col_at = col_at.astype(jnp.int32)
        starts = (zero_index, zero_index, row_at, col_at)
        window = lax.dynamic_slice(padded, starts, (2, SLICES, length, length))
        window = jnp.transpose(window, (1, 0, 2, 3)).astype(jnp.float32)
        gradient_window, pterm = position_terms(window, probe_modes[0], probe_modes[1], observed, tables)
        addend = jnp.transpose(gradient_window, (1, 0, 2, 3)).astype(jnp.float32)
        current = lax.dynamic_slice(grad_grid, starts, (2, SLICES, length, length))
        grad_grid = lax.dynamic_update_slice(grad_grid, current + addend, starts)
        return ((grad_grid, running + pterm), None)
    start_grid = jnp.zeros(padded.shape, jnp.float32)
    start_probe = jnp.zeros(probe_modes.shape, jnp.float32)
    (grad_grid, probe_grad), _ = lax.scan(advance, (start_grid, start_probe), (row_starts, col_starts, observed_all))
    object_grad = grad_grid[:, :, margin:margin + OH, margin:margin + OW]
    return (object_grad, probe_grad)
```

```python
import jax
import jax.numpy as jnp
import numpy as np
from jax import lax
from jax.experimental import pallas as pl
from jax.experimental.pallas import tpu as pltpu
from jax.sharding import PartitionSpec as P

prop_phase = 60.0
vmem_bytes = 48 * 1024 * 1024
f32 = jnp.float32
bf16 = jnp.bfloat16


def make_tables(length):
    indices = np.arange(length)
    angles = (indices[:, None] * indices[None, :] % length) * (2.0 * np.pi / length)
    cos = (np.cos(angles) / np.sqrt(length)).astype(np.float32)
    sin = (-np.sin(angles) / np.sqrt(length)).astype(np.float32)
    forward = np.block([[cos, sin], [-sin, cos]])
    inverse = np.block([[cos, -sin], [sin, cos]])
    shifted = (indices + length // 2) % length - length // 2
    frequency = shifted / length
    phases = -prop_phase * (frequency[:, None] ** 2 + frequency[None, :] ** 2)
    return (
        jnp.asarray(np.stack([forward, inverse])).astype(bf16),
        jnp.asarray(np.stack([np.cos(phases), np.sin(phases)]).astype(np.float32)),
    )


def with_halo(block, sides, width):
    for axis, dim in sides:
        count = lax.axis_size(axis)
        forward = [(i, i + 1) for i in range(count - 1)]
        backward = [(target, source) for source, target in forward]
        low = lax.ppermute(
            lax.slice_in_dim(block, block.shape[dim] - width, None, axis=dim), axis, forward
        )
        high = lax.ppermute(lax.slice_in_dim(block, 0, width, axis=dim), axis, backward)
        block = jnp.concatenate([low, block, high], axis=dim)
    return block


def ranks(tile_ref, first, per_dev):
    tiles = [tile_ref[first + q] for q in range(per_dev)]
    out = []
    for q in range(per_dev):
        rank = jnp.int32(0)
        for earlier in range(q):
            rank = rank + jnp.where(tiles[earlier] == tiles[q], 1, 0)
        out.append(rank)
    return tiles, out


def slot_place(refs, owner, slot, tile, per_dev):
    tile_ref, row_ref, col_ref = refs
    first = owner * per_dev
    tiles, order = ranks(tile_ref, first, per_dev)
    row, col, keep = jnp.int32(0), jnp.int32(0), jnp.int32(0)
    for q in range(per_dev):
        hit = jnp.where((tiles[q] == tile) & (order[q] == slot), 1, 0)
        row = row + hit * row_ref[first + q]
        col = col + hit * col_ref[first + q]
        keep = keep + hit
    return row, col, keep


def one_hot(shape, dim, shift, keep=None):
    wide = lax.broadcasted_iota(jnp.int32, shape, dim)
    narrow = lax.broadcasted_iota(jnp.int32, shape, 1 - dim)
    hit = wide == narrow + shift
    if keep is not None:
        hit = hit & (keep > 0)
    return jnp.where(hit, 1.0, 0.0).astype(bf16)


def dot(a, b):
    return jnp.dot(a, b, preferred_element_type=f32)


def column_base(col, width, length):
    return jnp.minimum(col // length * length, width - 2 * length)


def crop_kernel(per_dev, slots, tile_ref, row_ref, col_ref, padded_ref, out_ref):
    tile = lax.axis_index("tile")
    length = out_ref.shape[-1]
    _, rows, width = padded_ref.shape

    def body(index, carry):
        owner, slot = index // slots, index % slots
        row, col, _ = slot_place((tile_ref, row_ref, col_ref), owner, slot, tile, per_dev)
        base = column_base(col, width, length)
        pick_row = one_hot((length, rows), 1, row)
        pick_col = one_hot((2 * length, length), 0, col - base)
        for part in range(2):
            block = padded_ref[part, :, pl.ds(pl.multiple_of(base, length), 2 * length)]
            out_ref[index, part] = dot(dot(pick_row, block).astype(bf16), pick_col).astype(bf16)
        return carry

    lax.fori_loop(0, out_ref.shape[0], body, 0)


def scatter_kernel(per_dev, slots, tile_ref, row_ref, col_ref, back_ref, grid_ref):
    tile = lax.axis_index("tile")
    length = back_ref.shape[-1]
    _, rows, width = grid_ref.shape
    grid_ref[...] = jnp.zeros_like(grid_ref)

    def body(index, carry):
        owner, slot = index // slots, index % slots
        row, col, keep = slot_place((tile_ref, row_ref, col_ref), owner, slot, tile, per_dev)
        base = column_base(col, width, length)

        @pl.when(keep > 0)
        def _():
            put_row = one_hot((rows, length), 0, row)
            put_col = one_hot((length, 2 * length), 1, col - base)
            for part in range(2):
                where = pl.ds(pl.multiple_of(base, length), 2 * length)
                spread = dot(put_row, back_ref[index, part]).astype(bf16)
                grid_ref[part, :, where] += dot(spread, put_col)

        return carry

    lax.fori_loop(0, back_ref.shape[0], body, 0)


def split(field, length):
    modes = field.shape[1] // length
    return [
        (field[:length, m * length : (m + 1) * length], field[length:, m * length : (m + 1) * length])
        for m in range(modes)
    ]


def transform(fields, right, left, length):
    packed = jnp.concatenate(
        [jnp.concatenate([re.astype(bf16), im.astype(bf16)], axis=1) for re, im in fields], axis=0
    )
    mid = dot(packed, right).astype(bf16)
    turned = jnp.concatenate(
        [
            jnp.concatenate(
                [mid[m * length : (m + 1) * length, c * length : (c + 1) * length] for m in range(len(fields))],
                axis=1,
            )
            for c in range(2)
        ],
        axis=0,
    )
    return split(dot(left, turned), length)


def mul(a, b):
    return (a[0] * b[0] - a[1] * b[1], a[0] * b[1] + a[1] * b[0])


def conj_mul(a, b):
    return (a[0] * b[0] + a[1] * b[1], a[0] * b[1] - a[1] * b[0])


def total(pairs):
    return (sum(p[0] for p in pairs[1:]) + pairs[0][0], sum(p[1] for p in pairs[1:]) + pairs[0][1])


def position_terms(front, rear, probes, observed, tables, prop):
    length = observed.shape[0]
    ahead, behind = tables
    forward = lambda f: transform(f, ahead, behind, length)
    inverse = lambda f: transform(f, behind, ahead, length)
    spec = forward([mul(p, front) for p in probes])
    inner = inverse([mul(s, prop) for s in spec])
    far = forward([mul(s, rear) for s in inner])
    intensity = sum(re * re + im * im for re, im in far[1:]) + far[0][0] ** 2 + far[0][1] ** 2
    factor = 1.0 - jnp.sqrt(observed) / jnp.sqrt(intensity + 1.0)
    back_b = inverse([(re * factor, im * factor) for re, im in far])
    back_spec = forward([conj_mul(rear, b) for b in back_b])
    back_a = inverse([conj_mul(prop, b) for b in back_spec])
    grad_a = total([conj_mul(p, b) for p, b in zip(probes, back_a)])
    grad_b = total([conj_mul(s, b) for s, b in zip(inner, back_b)])
    return grad_a, grad_b, [conj_mul(front, b) for b in back_a]


def position_kernel(n_tile, n_mode, slots, tile_ref, arrived_ref, probe_ref, meas_ref, table_ref, prop_ref, back_ref, pgrad_ref):
    per_dev = meas_ref.shape[0]
    modes = probe_ref.shape[1]
    owner = lax.axis_index("tile") * n_mode + lax.axis_index("mode")
    tiles, order = ranks(tile_ref, owner * per_dev, per_dev)
    tables = (table_ref[0], table_ref[1])
    for q in range(per_dev):
        place = [(tiles[q] * n_mode + k * n_mode // 2) * slots + order[q] for k in range(2)]
        pair = lambda k: (arrived_ref[place[k], 0].astype(f32), arrived_ref[place[k], 1].astype(f32))
        probes = [(probe_ref[0, m], probe_ref[1, m]) for m in range(modes)]
        grad_a, grad_b, terms = position_terms(
            pair(0), pair(1), probes, meas_ref[q], tables, (prop_ref[0], prop_ref[1])
        )
        for k, grad in enumerate((grad_a, grad_b)):
            for part in range(2):
                back_ref[place[k], part] = grad[part].astype(bf16)
        for m, term in enumerate(terms):
            for part in range(2):
                if q == 0:
                    pgrad_ref[part, m] = term[part]
                else:
                    pgrad_ref[part, m] += term[part]


smem = pl.BlockSpec(memory_space=pltpu.SMEM)
vmem = pl.BlockSpec(memory_space=pltpu.VMEM)
params = pltpu.CompilerParams(vmem_limit_bytes=vmem_bytes)


def on_device(object_field, probe_modes, measured, pos_tile, off_row, off_col):
    length = probe_modes.shape[-1]
    margin = length // 2
    tile_rows = object_field.shape[2]
    tile_cols = object_field.shape[3]
    per_dev = measured.shape[1]
    n_tile = lax.axis_size("tile")
    n_mode = lax.axis_size("mode")
    slots = max(2, 2 * per_dev // n_tile)
    owners = n_tile * n_mode
    count = owners * slots
    tables, prop = make_tables(length)
    places = (pos_tile[0, :, 0], off_row[0], off_col[0])
    padded = with_halo(object_field[:, 0], (("tile", 2), ("strip", 1)), margin)
    windows = jax.ShapeDtypeStruct((count, 2, length, length), bf16)
    outgoing = pl.pallas_call(
        lambda *refs: crop_kernel(per_dev, slots, *refs),
        out_shape=windows,
        in_specs=[smem] * 3 + [vmem],
        out_specs=vmem,
        compiler_params=params,
        name="crop",
    )(*places, padded)
    arrived = lax.all_to_all(outgoing, ("tile", "mode"), split_axis=0, concat_axis=0, tiled=True)
    back, probe_part = pl.pallas_call(
        lambda *refs: position_kernel(n_tile, n_mode, slots, *refs),
        out_shape=(windows, jax.ShapeDtypeStruct(probe_modes.shape, f32)),
        in_specs=[smem] + [vmem] * 5,
        out_specs=(vmem, vmem),
        compiler_params=params,
        name="positions",
    )(places[0], arrived, probe_modes, measured[0], tables, prop)
    probe_grad = lax.psum(probe_part, ("tile", "strip", "mode"))
    returned = lax.all_to_all(back, ("tile", "mode"), split_axis=0, concat_axis=0, tiled=True)
    grid = pl.pallas_call(
        lambda *refs: scatter_kernel(per_dev, slots, *refs),
        out_shape=jax.ShapeDtypeStruct((2, tile_rows + 2 * margin, tile_cols + 2 * margin), f32),
        in_specs=[smem] * 3 + [vmem],
        out_specs=vmem,
        compiler_params=params,
        name="scatter",
    )(*places, returned)
    folded = fold(grid, "tile", 2, tile_cols, margin)
    folded = fold(folded, "strip", 1, tile_rows, margin)
    return (folded[:, None], probe_grad)


def fold(grid, axis, dim, count, width):
    steps = lax.axis_size(axis)
    forward = [(i, i + 1) for i in range(steps - 1)]
    backward = [(target, source) for source, target in forward]
    cut = lambda lo, hi: lax.slice_in_dim(grid, lo, hi, axis=dim)
    low = lax.ppermute(cut(count + width, count + 2 * width).astype(bf16), axis, forward)
    high = lax.ppermute(cut(0, width).astype(bf16), axis, backward)
    low_pad = [(0, 0)] * grid.ndim
    high_pad = [(0, 0)] * grid.ndim
    low_pad[dim] = (0, count - width)
    high_pad[dim] = (count - width, 0)
    return (
        cut(width, width + count)
        + jnp.pad(low.astype(f32), low_pad)
        + jnp.pad(high.astype(f32), high_pad)
    )


def solution(mesh):
    return jax.shard_map(
        on_device,
        mesh=mesh,
        in_specs=(
            P("group", "mode", "strip", "tile"),
            P("group", None, None, None),
            P(("group", "strip"), ("tile", "mode"), None, None),
            P(("group", "strip"), None, None),
            P(("group", "strip"), None),
            P(("group", "strip"), None),
        ),
        out_specs=(P("group", "mode", "strip", "tile"), P("group", None, None, None)),
        check_vma=False,
    )
```

```python
import jax
import jax.numpy as jnp
import numpy as np
from jax import lax
from jax.experimental import pallas as pl
from jax.experimental.pallas import tpu as pltpu
from jax.sharding import PartitionSpec as P

prop_phase = 60.0
vmem_bytes = 48 * 1024 * 1024
f32 = jnp.float32
bf16 = jnp.bfloat16


def make_tables(length):
    indices = np.arange(length)
    angles = (indices[:, None] * indices[None, :] % length) * (2.0 * np.pi / length)
    cos = (np.cos(angles) / np.sqrt(length)).astype(np.float32)
    sin = (-np.sin(angles) / np.sqrt(length)).astype(np.float32)
    forward = np.block([[cos, sin], [-sin, cos]])
    inverse = np.block([[cos, -sin], [sin, cos]])
    shifted = (indices + length // 2) % length - length // 2
    frequency = shifted / length
    phases = -prop_phase * (frequency[:, None] ** 2 + frequency[None, :] ** 2)
    return (
        jnp.asarray(np.stack([forward, inverse])).astype(bf16),
        jnp.asarray(np.stack([np.cos(phases), np.sin(phases)]).astype(np.float32)),
    )


def ranks(tile_ref, first, per_dev):
    tiles = [tile_ref[first + q] for q in range(per_dev)]
    out = []
    for q in range(per_dev):
        rank = jnp.int32(0)
        for earlier in range(q):
            rank = rank + jnp.where(tiles[earlier] == tiles[q], 1, 0)
        out.append(rank)
    return tiles, out


def slot_place(refs, owner, slot, tile, per_dev):
    tile_ref, row_ref, col_ref = refs
    first = owner * per_dev
    tiles, order = ranks(tile_ref, first, per_dev)
    row, col, keep = jnp.int32(0), jnp.int32(0), jnp.int32(0)
    for q in range(per_dev):
        hit = jnp.where((tiles[q] == tile) & (order[q] == slot), 1, 0)
        row = row + hit * row_ref[first + q]
        col = col + hit * col_ref[first + q]
        keep = keep + hit
    return row, col, keep


def one_hot(shape, dim, shift, keep=None):
    wide = lax.broadcasted_iota(jnp.int32, shape, dim)
    narrow = lax.broadcasted_iota(jnp.int32, shape, 1 - dim)
    hit = wide == narrow + shift
    if keep is not None:
        hit = hit & (keep > 0)
    return jnp.where(hit, 1.0, 0.0).astype(bf16)


def dot(a, b):
    return jnp.dot(a, b, preferred_element_type=f32)


def remote(src, dst, send, recv, device):
    return pltpu.make_async_remote_copy(
        src_ref=src,
        dst_ref=dst,
        send_sem=send,
        recv_sem=recv,
        device_id=device,
        device_id_type=pl.DeviceIdType.MESH,
    )


def owner_id(owner, n_mode):
    return {"tile": owner // n_mode, "mode": owner % n_mode}


def others(me, count, act, start=None):
    first = count // 2 if start is None else start

    def body(step, carry):
        other = lax.rem(me + first + step, count)

        @pl.when(other != me)
        def _():
            act(other)

        return carry

    lax.fori_loop(0, count, body, 0)


def greet(me, owners, n_mode, strip, n_strip, neighbours_only):
    barrier = pltpu.get_barrier_semaphore()

    def call(device):
        pl.semaphore_signal(barrier, inc=1, device_id=device, device_id_type=pl.DeviceIdType.MESH)

    others(me, owners, lambda other: call(owner_id(other, n_mode)))
    if neighbours_only:
        pl.when(strip > 0)(lambda: call({"strip": strip - 1}))
        pl.when(strip < n_strip - 1)(lambda: call({"strip": strip + 1}))
        beside = jnp.minimum(strip, 1) + jnp.minimum(n_strip - 1 - strip, 1)
        pl.semaphore_wait(barrier, owners - 1 + beside)
    else:
        others(strip, n_strip, lambda other: call({"strip": other}))
        pl.semaphore_wait(barrier, owners + n_strip - 2)


def swap(axis, here, count, up, down, sends, recvs):
    to_next = remote(*up, sends.at[0], recvs.at[0], {axis: here + 1})
    to_prev = remote(*down, sends.at[1], recvs.at[1], {axis: here - 1})
    has_next, has_prev = here < count - 1, here > 0

    def start():
        pl.when(has_next)(to_next.start)
        pl.when(has_prev)(to_prev.start)

    def wait():
        @pl.when(has_next)
        def _():
            to_next.wait_send()
            remote(*down, sends.at[1], recvs.at[1], {axis: here + 1}).wait_recv()

        @pl.when(has_prev)
        def _():
            to_prev.wait_send()
            remote(*up, sends.at[0], recvs.at[0], {axis: here - 1}).wait_recv()

    return start, wait, has_next, has_prev


def forward_kernel(
    per_dev, slots, n_tile, n_mode, n_strip, margin,
    tile_ref, row_ref, col_ref, object_ref, arrived_ref,
    padded_ref, out_ref, tile_send, tile_recv, strip_send, strip_recv, send_sem, recv_sem,
):
    tile, mode, strip = (lax.axis_index(axis) for axis in ("tile", "mode", "strip"))
    me, owners = tile * n_mode + mode, n_tile * n_mode
    length = out_ref.shape[-1]
    _, tile_rows, tile_cols = object_ref.shape
    _, rows, width = padded_ref.shape
    own_rows = pl.ds(margin, tile_rows)
    greet(me, owners, n_mode, strip, n_strip, True)
    start, wait, has_next, has_prev = swap(
        "tile", tile, n_tile,
        (object_ref.at[:, :, pl.ds(tile_cols - length, length)], padded_ref.at[:, own_rows, pl.ds(0, length)]),
        (object_ref.at[:, :, pl.ds(0, length)], padded_ref.at[:, own_rows, pl.ds(width - length, length)]),
        tile_send, tile_recv,
    )
    start()
    padded_ref[:, own_rows, pl.ds(length, tile_cols)] = object_ref[...]
    edge = jnp.zeros((2, tile_rows, length), bf16)
    flat = jnp.zeros((2, margin, width), bf16)

    @pl.when(jnp.logical_not(has_prev))
    def _():
        padded_ref[:, own_rows, pl.ds(0, length)] = edge

    @pl.when(jnp.logical_not(has_next))
    def _():
        padded_ref[:, own_rows, pl.ds(width - length, length)] = edge

    wait()
    start, wait, has_next, has_prev = swap(
        "strip", strip, n_strip,
        (padded_ref.at[:, pl.ds(tile_rows, margin), :], padded_ref.at[:, pl.ds(0, margin), :]),
        (padded_ref.at[:, pl.ds(margin, margin), :], padded_ref.at[:, pl.ds(tile_rows + margin, margin), :]),
        strip_send, strip_recv,
    )
    start()

    @pl.when(jnp.logical_not(has_prev))
    def _():
        padded_ref[:, pl.ds(0, margin), :] = flat

    @pl.when(jnp.logical_not(has_next))
    def _():
        padded_ref[:, pl.ds(tile_rows + margin, margin), :] = flat

    wait()

    def span(owner):
        return pl.ds(owner * slots, slots)

    def body(step, carry):
        owner = lax.rem(me + owners // 2 + step, owners)
        for slot in range(slots):
            row, col, _ = slot_place((tile_ref, row_ref, col_ref), owner, slot, tile, per_dev)
            col = col + margin
            pick_row = one_hot((length, rows), 1, row)
            pick_col = one_hot((width, length), 0, col)
            for part in range(2):
                window = dot(dot(pick_row, padded_ref[part]).astype(bf16), pick_col)
                out_ref[owner * slots + slot, part] = window.astype(bf16)

        @pl.when(owner != me)
        def _():
            remote(
                out_ref.at[span(owner)], arrived_ref.at[span(me)],
                send_sem.at[owner], recv_sem.at[me], owner_id(owner, n_mode),
            ).start()

        return carry

    lax.fori_loop(0, owners, body, 0)
    arrived_ref[span(me)] = out_ref[span(me)]

    def finish(other):
        copy = remote(
            out_ref.at[span(other)], arrived_ref.at[span(other)],
            send_sem.at[other], recv_sem.at[other], owner_id(other, n_mode),
        )
        copy.wait_send()
        copy.wait_recv()

    others(me, owners, finish)


def backward_kernel(
    per_dev, slots, n_tile, n_mode, n_strip, margin,
    tile_ref, row_ref, col_ref, back_ref, part_ref, object_ref, probe_ref,
    returned_ref, grid_ref, spread_ref, put_ref, rs_ref, sum_ref, strip_ref,
    col_out, col_in, row_out, row_in,
    send_sem, recv_sem, rs_send, rs_recv, st_send, st_recv, ag_send, ag_recv,
    tile_send, tile_recv, strip_send, strip_recv,
):
    tile, mode, strip = (lax.axis_index(axis) for axis in ("tile", "mode", "strip"))
    me, owners = tile * n_mode + mode, n_tile * n_mode
    count = owners * slots
    length = back_ref.shape[-1]
    _, tile_rows, tile_cols = object_ref.shape
    _, rows, width = grid_ref.shape
    piece = rs_ref.shape[1]
    greet(me, owners, n_mode, strip, n_strip, False)

    def span(owner):
        return pl.ds(owner * slots, slots)

    def share(owner):
        return pl.ds(pl.multiple_of(owner * piece, piece), piece)

    def reduce_copy(other, source):
        return remote(
            part_ref.at[share(other)], rs_ref.at[source],
            rs_send.at[other], rs_recv.at[source], owner_id(other, n_mode),
        )

    def window_copy(other, source):
        return remote(
            back_ref.at[span(other)], returned_ref.at[span(source)],
            send_sem.at[other], recv_sem.at[source], owner_id(other, n_mode),
        )

    def strip_copy(other, source):
        return remote(
            sum_ref, strip_ref.at[source], st_send.at[other], st_recv.at[source], {"strip": other}
        )

    def gather_copy(other, source):
        return remote(
            probe_ref.at[share(me)], probe_ref.at[share(source)],
            ag_send.at[other], ag_recv.at[source], owner_id(other, n_mode),
        )

    def finish(make):
        def act(other):
            make(other, other).wait_send()
            make(other, other).wait_recv()

        return act

    others(me, owners, lambda other: reduce_copy(other, me).start())
    others(me, owners, lambda other: window_copy(other, me).start())
    rs_ref[me] = part_ref[share(me)]
    returned_ref[span(me)] = back_ref[span(me)]
    refs = (tile_ref, row_ref, col_ref)

    def build(index, carry):
        _, col, _ = slot_place(refs, index // slots, index % slots, tile, per_dev)
        where = pl.ds(pl.multiple_of(index * length, length), length)
        put_ref[where, :] = one_hot((length, width), 1, col + margin)
        return carry

    lax.fori_loop(0, count, build, 0)
    others(me, owners, finish(reduce_copy))
    sum_ref[...] = lax.fori_loop(1, owners, lambda i, acc: acc + rs_ref[i], rs_ref[0])
    others(strip, n_strip, lambda other: strip_copy(other, strip).start())
    strip_ref[strip] = sum_ref[...]
    others(strip, n_strip, finish(strip_copy))
    probe_ref[share(me)] = lax.fori_loop(1, n_strip, lambda i, acc: acc + strip_ref[i], strip_ref[0])
    others(me, owners, lambda other: gather_copy(other, me).start())
    others(me, owners, finish(window_copy))

    def place(index, carry):
        row, _, keep = slot_place(refs, index // slots, index % slots, tile, per_dev)
        where = pl.ds(pl.multiple_of(index * length, length), length)
        put_row = one_hot((rows, length), 0, row, keep)
        for part in range(2):
            spread_ref[part, :, where] = dot(put_row, returned_ref[index, part]).astype(bf16)
        return carry

    lax.fori_loop(0, count, place, 0)

    def fill(block, carry):
        where = pl.ds(pl.multiple_of(block * 2 * length, 2 * length), 2 * length)
        for part in range(2):
            grid_ref[part, :, where] = dot(spread_ref[part], put_ref[:, where])
        return carry

    lax.fori_loop(0, width // (2 * length), fill, 0)
    col_out[0] = grid_ref[:, :, pl.ds(width - length, length)].astype(bf16)
    col_out[1] = grid_ref[:, :, pl.ds(0, length)].astype(bf16)
    start, wait, has_next, has_prev = swap(
        "tile", tile, n_tile,
        (col_out.at[0], col_in.at[0]), (col_out.at[1], col_in.at[1]), tile_send, tile_recv,
    )
    start()
    wait()

    @pl.when(has_prev)
    def _():
        grid_ref[:, :, pl.ds(length, length)] += col_in[0].astype(f32)

    @pl.when(has_next)
    def _():
        grid_ref[:, :, pl.ds(width - 2 * length, length)] += col_in[1].astype(f32)

    own = pl.ds(length, tile_cols)
    row_out[0] = grid_ref[:, pl.ds(margin + tile_rows, margin), own].astype(bf16)
    row_out[1] = grid_ref[:, pl.ds(0, margin), own].astype(bf16)
    start, wait, has_next, has_prev = swap(
        "strip", strip, n_strip,
        (row_out.at[0], row_in.at[0]), (row_out.at[1], row_in.at[1]), strip_send, strip_recv,
    )
    start()
    object_ref[...] = grid_ref[:, pl.ds(margin, tile_rows), own]
    wait()

    @pl.when(has_prev)
    def _():
        object_ref[:, pl.ds(0, margin), :] += row_in[0].astype(f32)

    @pl.when(has_next)
    def _():
        object_ref[:, pl.ds(tile_rows - margin, margin), :] += row_in[1].astype(f32)

    others(me, owners, finish(gather_copy))


def split(field, length):
    modes = field.shape[1] // length
    return [
        (field[:length, m * length : (m + 1) * length], field[length:, m * length : (m + 1) * length])
        for m in range(modes)
    ]


def transform(fields, right, left, length):
    packed = jnp.concatenate(
        [jnp.concatenate([re.astype(bf16), im.astype(bf16)], axis=1) for re, im in fields], axis=0
    )
    mid = dot(packed, right).astype(bf16)
    turned = jnp.concatenate(
        [
            jnp.concatenate(
                [mid[m * length : (m + 1) * length, c * length : (c + 1) * length] for m in range(len(fields))],
                axis=1,
            )
            for c in range(2)
        ],
        axis=0,
    )
    return split(dot(left, turned), length)


def mul(a, b):
    return (a[0] * b[0] - a[1] * b[1], a[0] * b[1] + a[1] * b[0])


def conj_mul(a, b):
    return (a[0] * b[0] + a[1] * b[1], a[0] * b[1] - a[1] * b[0])


def total(pairs):
    return (sum(p[0] for p in pairs[1:]) + pairs[0][0], sum(p[1] for p in pairs[1:]) + pairs[0][1])


def position_terms(front, rear, probes, observed, tables, prop):
    length = observed.shape[0]
    ahead, behind = tables
    forward = lambda f: transform(f, ahead, behind, length)
    inverse = lambda f: transform(f, behind, ahead, length)
    spec = forward([mul(p, front) for p in probes])
    inner = inverse([mul(s, prop) for s in spec])
    far = forward([mul(s, rear) for s in inner])
    intensity = sum(re * re + im * im for re, im in far[1:]) + far[0][0] ** 2 + far[0][1] ** 2
    factor = 1.0 - jnp.sqrt(observed) / jnp.sqrt(intensity + 1.0)
    back_b = inverse([(re * factor, im * factor) for re, im in far])
    back_spec = forward([conj_mul(rear, b) for b in back_b])
    back_a = inverse([conj_mul(prop, b) for b in back_spec])
    grad_a = total([conj_mul(p, b) for p, b in zip(probes, back_a)])
    grad_b = total([conj_mul(s, b) for s, b in zip(inner, back_b)])
    return grad_a, grad_b, [conj_mul(front, b) for b in back_a]


def position_kernel(n_tile, n_mode, slots, tile_ref, arrived_ref, probe_ref, meas_ref, table_ref, prop_ref, back_ref, pgrad_ref):
    per_dev = meas_ref.shape[0]
    modes = probe_ref.shape[1]
    owner = lax.axis_index("tile") * n_mode + lax.axis_index("mode")
    tiles, order = ranks(tile_ref, owner * per_dev, per_dev)
    tables = (table_ref[0], table_ref[1])
    back_ref[...] = jnp.zeros_like(back_ref)
    for q in range(per_dev):
        place = [(tiles[q] * n_mode + k * n_mode // 2) * slots + order[q] for k in range(2)]
        pair = lambda k: (arrived_ref[place[k], 0].astype(f32), arrived_ref[place[k], 1].astype(f32))
        probes = [(probe_ref[0, m], probe_ref[1, m]) for m in range(modes)]
        grad_a, grad_b, terms = position_terms(
            pair(0), pair(1), probes, meas_ref[q], tables, (prop_ref[0], prop_ref[1])
        )
        for k, grad in enumerate((grad_a, grad_b)):
            for part in range(2):
                back_ref[place[k], part] = grad[part].astype(bf16)
        for m, term in enumerate(terms):
            for part in range(2):
                if q == 0:
                    pgrad_ref[part, m] = term[part]
                else:
                    pgrad_ref[part, m] += term[part]


smem = pl.BlockSpec(memory_space=pltpu.SMEM)
vmem = pl.BlockSpec(memory_space=pltpu.VMEM)
params = pltpu.CompilerParams(vmem_limit_bytes=vmem_bytes)


def communicating(number):
    return pltpu.CompilerParams(
        vmem_limit_bytes=vmem_bytes, collective_id=number, has_side_effects=True
    )


def on_device(object_field, probe_modes, measured, pos_tile, off_row, off_col):
    length = probe_modes.shape[-1]
    margin = length // 2
    tile_rows = object_field.shape[2]
    tile_cols = object_field.shape[3]
    per_dev = measured.shape[1]
    n_tile = lax.axis_size("tile")
    n_mode = lax.axis_size("mode")
    slots = max(2, 2 * per_dev // n_tile)
    owners = n_tile * n_mode
    count = owners * slots
    tables, prop = make_tables(length)
    places = (pos_tile[0, :, 0], off_row[0], off_col[0])
    n_strip = lax.axis_size("strip")
    sizes = (per_dev, slots, n_tile, n_mode, n_strip, margin)
    windows = jax.ShapeDtypeStruct((count, 2, length, length), bf16)
    rows, width = tile_rows + 2 * margin, tile_cols + 2 * length
    dma = pltpu.SemaphoreType.DMA
    arrived = pl.pallas_call(
        lambda *refs: forward_kernel(*sizes, *refs),
        out_shape=windows,
        in_specs=[smem] * 3 + [vmem],
        out_specs=vmem,
        scratch_shapes=[
            pltpu.VMEM((2, rows, width), bf16),
            pltpu.VMEM(windows.shape, bf16),
            *[dma((2,))] * 4,
            *[dma((owners,))] * 2,
        ],
        compiler_params=communicating(0),
        name="forward",
    )(*places, object_field[:, 0])
    back, probe_part = pl.pallas_call(
        lambda *refs: position_kernel(n_tile, n_mode, slots, *refs),
        out_shape=(windows, jax.ShapeDtypeStruct(probe_modes.shape, f32)),
        in_specs=[smem] + [vmem] * 5,
        out_specs=(vmem, vmem),
        compiler_params=params,
        name="positions",
    )(places[0], arrived, probe_modes, measured[0], tables, prop)
    flat = probe_part.reshape(-1, length)
    piece = flat.shape[0] // owners
    object_grad, probe_grad = pl.pallas_call(
        lambda *refs: backward_kernel(*sizes, *refs),
        out_shape=(
            jax.ShapeDtypeStruct((2, tile_rows, tile_cols), f32),
            jax.ShapeDtypeStruct(flat.shape, f32),
        ),
        in_specs=[smem] * 3 + [vmem] * 2,
        out_specs=(vmem, vmem),
        scratch_shapes=[
            pltpu.VMEM(windows.shape, bf16),
            pltpu.VMEM((2, rows, width), f32),
            pltpu.VMEM((2, rows, count * length), bf16),
            pltpu.VMEM((count * length, width), bf16),
            pltpu.VMEM((owners, piece, length), f32),
            pltpu.VMEM((piece, length), f32),
            pltpu.VMEM((n_strip, piece, length), f32),
            *[pltpu.VMEM((2, 2, rows, length), bf16)] * 2,
            *[pltpu.VMEM((2, 2, margin, tile_cols), bf16)] * 2,
            *[dma((owners,))] * 4,
            *[dma((n_strip,))] * 2,
            *[dma((owners,))] * 2,
            *[dma((2,))] * 4,
        ],
        compiler_params=communicating(1),
        name="backward",
    )(*places, back, flat)
    return (object_grad[:, None], probe_grad.reshape(probe_modes.shape))


def solution(mesh):
    return jax.shard_map(
        on_device,
        mesh=mesh,
        in_specs=(
            P("group", "mode", "strip", "tile"),
            P("group", None, None, None),
            P(("group", "strip"), ("tile", "mode"), None, None),
            P(("group", "strip"), None, None),
            P(("group", "strip"), None),
            P(("group", "strip"), None),
        ),
        out_specs=(P("group", "mode", "strip", "tile"), P("group", None, None, None)),
        check_vma=False,
    )
```

```python
import jax
import jax.numpy as jnp
import numpy as np
from jax import lax
from jax.experimental import pallas as pl
from jax.experimental.pallas import tpu as pltpu
from jax.sharding import PartitionSpec as P

prop_phase = 60.0
vmem_bytes = 48 * 1024 * 1024
f32 = jnp.float32
bf16 = jnp.bfloat16


def make_tables(length):
    indices = np.arange(length)
    angles = (indices[:, None] * indices[None, :] % length) * (2.0 * np.pi / length)
    cos = (np.cos(angles) / np.sqrt(length)).astype(np.float32)
    sin = (-np.sin(angles) / np.sqrt(length)).astype(np.float32)
    forward = np.block([[cos, sin], [-sin, cos]])
    inverse = np.block([[cos, -sin], [sin, cos]])
    shifted = (indices + length // 2) % length - length // 2
    frequency = shifted / length
    phases = -prop_phase * (frequency[:, None] ** 2 + frequency[None, :] ** 2)
    return (
        jnp.asarray(np.stack([forward, inverse])).astype(bf16),
        jnp.asarray(np.stack([np.cos(phases), np.sin(phases)]).astype(np.float32)),
    )


def ranks(tile_ref, first, per_dev):
    tiles = [tile_ref[first + q] for q in range(per_dev)]
    out = []
    for q in range(per_dev):
        rank = jnp.int32(0)
        for earlier in range(q):
            rank = rank + jnp.where(tiles[earlier] == tiles[q], 1, 0)
        out.append(rank)
    return tiles, out


def slot_place(refs, owner, slot, tile, per_dev):
    tile_ref, row_ref, col_ref = refs
    first = owner * per_dev
    tiles, order = ranks(tile_ref, first, per_dev)
    row, col, keep = jnp.int32(0), jnp.int32(0), jnp.int32(0)
    for q in range(per_dev):
        hit = jnp.where((tiles[q] == tile) & (order[q] == slot), 1, 0)
        row = row + hit * row_ref[first + q]
        col = col + hit * col_ref[first + q]
        keep = keep + hit
    return row, col, keep


def one_hot(shape, dim, shift, keep=None):
    wide = lax.broadcasted_iota(jnp.int32, shape, dim)
    narrow = lax.broadcasted_iota(jnp.int32, shape, 1 - dim)
    hit = wide == narrow + shift
    if keep is not None:
        hit = hit & (keep > 0)
    return jnp.where(hit, 1.0, 0.0).astype(bf16)


def dot(a, b):
    return jnp.dot(a, b, preferred_element_type=f32)


def remote(src, dst, send, recv, device):
    return pltpu.make_async_remote_copy(
        src_ref=src,
        dst_ref=dst,
        send_sem=send,
        recv_sem=recv,
        device_id=device,
        device_id_type=pl.DeviceIdType.MESH,
    )


def owner_id(owner, n_mode):
    return {"tile": owner // n_mode, "mode": owner % n_mode}


def others(me, count, act, start=None):
    first = count // 2 if start is None else start

    def body(step, carry):
        other = lax.rem(me + first + step, count)

        @pl.when(other != me)
        def _():
            act(other)

        return carry

    lax.fori_loop(0, count, body, 0)


directions = [(dt, ds) for ds in (-1, 0, 1) for dt in (-1, 0, 1) if (dt, ds) != (0, 0)]


def exists(here, count, step):
    if step == 0:
        return jnp.int32(1)
    return jnp.minimum(count - 1 - here if step > 0 else here, 1)


def neighbour(spot, direction, sign):
    tile, strip, n_tile, n_strip = spot
    dt, ds = (sign * d for d in direction)
    there = exists(tile, n_tile, dt) * exists(strip, n_strip, ds)
    return there, {"tile": tile + dt, "strip": strip + ds}


def greet(me, owners, n_mode, spot):
    barrier = pltpu.get_barrier_semaphore()
    tile, strip, n_tile, n_strip = spot

    def call(device):
        pl.semaphore_signal(barrier, inc=1, device_id=device, device_id_type=pl.DeviceIdType.MESH)

    others(me, owners, lambda other: call(owner_id(other, n_mode)))
    others(strip, n_strip, lambda other: call({"strip": other}))
    amount = owners + n_strip - 2
    for direction in directions:
        if 0 not in direction:
            there, device = neighbour(spot, direction, 1)
            pl.when(there > 0)(lambda: call(device))
            amount = amount + there
    pl.semaphore_wait(barrier, amount)


def side(step, before, middle, after):
    return ((0, before), (before, middle), (before + middle, after))[step + 1]


def margin_part(ref, dt, ds, tile_rows, tile_cols, margin, length):
    row, row_count = side(ds, margin, tile_rows, margin)
    col, col_count = side(dt, length, tile_cols, length)
    return ref.at[:, pl.ds(row, row_count), pl.ds(col, col_count)]


def forward_kernel(
    per_dev, slots, n_tile, n_mode, n_strip, margin,
    tile_ref, row_ref, col_ref, object_ref, arrived_ref,
    padded_ref, out_ref, halo_send, halo_recv, send_sem, recv_sem,
):
    tile, mode, strip = (lax.axis_index(axis) for axis in ("tile", "mode", "strip"))
    me, owners = tile * n_mode + mode, n_tile * n_mode
    length = out_ref.shape[-1]
    _, tile_rows, tile_cols = object_ref.shape
    _, rows, width = padded_ref.shape
    spot = (tile, strip, n_tile, n_strip)
    greet(me, owners, n_mode, spot)

    def edge(dt, ds):
        row = {1: tile_rows - margin}.get(ds, 0)
        col = {1: tile_cols - length}.get(dt, 0)
        return object_ref.at[
            :, pl.ds(row, margin if ds else tile_rows), pl.ds(col, length if dt else tile_cols)
        ]

    def region(dt, ds):
        return margin_part(padded_ref, dt, ds, tile_rows, tile_cols, margin, length)

    def halo(number, sign):
        dt, ds = directions[number]
        there, device = neighbour(spot, (dt, ds), sign)
        copy = remote(edge(dt, ds), region(-dt, -ds), halo_send.at[number], halo_recv.at[number], device)
        return there, copy

    for number in range(len(directions)):
        there, copy = halo(number, 1)
        pl.when(there > 0)(copy.start)
    region(0, 0)[...] = object_ref[...]
    for number, (dt, ds) in enumerate(directions):
        there, _ = neighbour(spot, (dt, ds), -1)
        target = region(-dt, -ds)

        @pl.when(there == 0)
        def _():
            target[...] = jnp.zeros(target.shape, bf16)

    for number in range(len(directions)):
        there, copy = halo(number, 1)
        pl.when(there > 0)(copy.wait_send)
        there, copy = halo(number, -1)
        pl.when(there > 0)(copy.wait_recv)

    def span(owner):
        return pl.ds(owner * slots, slots)

    def body(step, carry):
        owner = lax.rem(me + owners // 2 + step, owners)
        for slot in range(slots):
            row, col, _ = slot_place((tile_ref, row_ref, col_ref), owner, slot, tile, per_dev)
            col = col + margin
            pick_row = one_hot((length, rows), 1, row)
            pick_col = one_hot((width, length), 0, col)
            for part in range(2):
                window = dot(dot(pick_row, padded_ref[part]).astype(bf16), pick_col)
                out_ref[owner * slots + slot, part] = window.astype(bf16)

        @pl.when(owner != me)
        def _():
            remote(
                out_ref.at[span(owner)], arrived_ref.at[span(me)],
                send_sem.at[owner], recv_sem.at[me], owner_id(owner, n_mode),
            ).start()

        return carry

    lax.fori_loop(0, owners, body, 0)
    arrived_ref[span(me)] = out_ref[span(me)]

    def finish(other):
        copy = remote(
            out_ref.at[span(other)], arrived_ref.at[span(other)],
            send_sem.at[other], recv_sem.at[other], owner_id(other, n_mode),
        )
        copy.wait_send()
        copy.wait_recv()

    others(me, owners, finish)


def backward_kernel(
    per_dev, slots, n_tile, n_mode, n_strip, margin,
    tile_ref, row_ref, col_ref, back_ref, part_ref, object_ref, probe_ref,
    returned_ref, grid_ref, spread_ref, put_ref, pair_ref, half_ref, rs_ref, sum_ref, strip_ref,
    margin_out, margin_in,
    send_sem, recv_sem, pair_send, pair_recv, rs_send, rs_recv, st_send, st_recv,
    ag_send, ag_recv, join_send, join_recv, margin_send, margin_recv,
):
    tile, mode, strip = (lax.axis_index(axis) for axis in ("tile", "mode", "strip"))
    me, owners = tile * n_mode + mode, n_tile * n_mode
    count = owners * slots
    length = back_ref.shape[-1]
    _, tile_rows, tile_cols = object_ref.shape
    _, rows, width = grid_ref.shape
    piece = rs_ref.shape[1]
    half = n_tile * piece
    spot = (tile, strip, n_tile, n_strip)
    greet(me, owners, n_mode, spot)

    def span(owner):
        return pl.ds(owner * slots, slots)

    def share(index, size):
        return pl.ds(pl.multiple_of(index * size, piece), size)

    def pair_copy(other, source):
        return remote(
            part_ref.at[share(other, half)], pair_ref.at[source],
            pair_send.at[other], pair_recv.at[source], {"mode": other},
        )

    def reduce_copy(other, source):
        return remote(
            half_ref.at[share(other, piece)], rs_ref.at[source],
            rs_send.at[other], rs_recv.at[source], {"tile": other},
        )

    def window_copy(other, source):
        return remote(
            back_ref.at[span(other)], returned_ref.at[span(source)],
            send_sem.at[other], recv_sem.at[source], owner_id(other, n_mode),
        )

    def strip_copy(other, source):
        return remote(
            sum_ref, strip_ref.at[source], st_send.at[other], st_recv.at[source], {"strip": other}
        )

    def gather_copy(other, source):
        return remote(
            probe_ref.at[share(mode * n_tile + tile, piece)],
            probe_ref.at[share(mode * n_tile + source, piece)],
            ag_send.at[other], ag_recv.at[source], {"tile": other},
        )

    def join_copy(other, source):
        return remote(
            probe_ref.at[share(mode, half)], probe_ref.at[share(source, half)],
            join_send.at[other], join_recv.at[source], {"mode": other},
        )

    def finish(make):
        def act(other):
            make(other, other).wait_send()
            make(other, other).wait_recv()

        return act

    others(mode, n_mode, lambda other: pair_copy(other, mode).start())
    others(me, owners, lambda other: window_copy(other, me).start())
    pair_ref[mode] = part_ref[share(mode, half)]
    returned_ref[span(me)] = back_ref[span(me)]
    others(mode, n_mode, finish(pair_copy))
    half_ref[...] = lax.fori_loop(1, n_mode, lambda i, acc: acc + pair_ref[i], pair_ref[0])
    others(tile, n_tile, lambda other: reduce_copy(other, tile).start())
    rs_ref[tile] = half_ref[share(tile, piece)]
    refs = (tile_ref, row_ref, col_ref)

    def build(index, carry):
        _, col, _ = slot_place(refs, index // slots, index % slots, tile, per_dev)
        where = pl.ds(pl.multiple_of(index * length, length), length)
        put_ref[where, :] = one_hot((length, width), 1, col + margin)
        return carry

    lax.fori_loop(0, count, build, 0)
    others(tile, n_tile, finish(reduce_copy))
    sum_ref[...] = lax.fori_loop(1, n_tile, lambda i, acc: acc + rs_ref[i], rs_ref[0])
    others(strip, n_strip, lambda other: strip_copy(other, strip).start())
    strip_ref[strip] = sum_ref[...]
    others(strip, n_strip, finish(strip_copy))
    probe_ref[share(mode * n_tile + tile, piece)] = lax.fori_loop(
        1, n_strip, lambda i, acc: acc + strip_ref[i], strip_ref[0]
    )
    others(tile, n_tile, lambda other: gather_copy(other, tile).start())

    def place(step, carry):
        owner = lax.rem(me + 2 * owners - owners // 2 - step, owners)

        @pl.when(owner != me)
        def _():
            finish(window_copy)(owner)

        for slot in range(slots):
            index = owner * slots + slot
            row, _, keep = slot_place(refs, owner, slot, tile, per_dev)
            where = pl.ds(pl.multiple_of(index * length, length), length)
            put_row = one_hot((rows, length), 0, row, keep)
            for part in range(2):
                spread_ref[part, :, where] = dot(put_row, returned_ref[index, part]).astype(bf16)
        return carry

    lax.fori_loop(0, owners, place, 0)

    def fill(col, size):
        where = pl.ds(col, size)
        for part in range(2):
            grid_ref[part, :, where] = dot(spread_ref[part], put_ref[:, where])

    def region(ref, dt, ds):
        return margin_part(ref, dt, ds, tile_rows, tile_cols, margin, length)

    def margin_copy(number, sign):
        dt, ds = directions[number]
        there, device = neighbour(spot, (dt, ds), sign)
        copy = remote(
            region(margin_out, dt, ds), region(margin_in, -dt, -ds),
            margin_send.at[number], margin_recv.at[number], device,
        )
        return there, copy

    def send_margins(columns):
        for number, (dt, ds) in enumerate(directions):
            if (dt != 0) == columns:
                region(margin_out, dt, ds)[...] = region(grid_ref, dt, ds)[...].astype(bf16)
                there, copy = margin_copy(number, 1)
                pl.when(there > 0)(copy.start)

    fill(0, 2 * length)
    fill(width - 2 * length, 2 * length)
    send_margins(True)
    fill(2 * length, width - 4 * length)
    send_margins(False)
    others(tile, n_tile, finish(gather_copy))
    others(mode, n_mode, lambda other: join_copy(other, mode).start())
    object_ref[...] = region(grid_ref, 0, 0)[...]
    for number, (dt, ds) in enumerate(directions):
        there, copy = margin_copy(number, 1)
        pl.when(there > 0)(copy.wait_send)
        there, copy = margin_copy(number, -1)
        row = {-1: tile_rows - margin}.get(ds, 0)
        col = {-1: tile_cols - length}.get(dt, 0)
        target = object_ref.at[
            :, pl.ds(row, margin if ds else tile_rows), pl.ds(col, length if dt else tile_cols)
        ]
        arriving = region(margin_in, -dt, -ds)

        @pl.when(there > 0)
        def _():
            copy.wait_recv()
            target[...] += arriving[...].astype(f32)

    others(mode, n_mode, finish(join_copy))


def split(field, length):
    modes = field.shape[1] // length
    return [
        (field[:length, m * length : (m + 1) * length], field[length:, m * length : (m + 1) * length])
        for m in range(modes)
    ]


def transform(fields, right, left, length):
    packed = jnp.concatenate(
        [jnp.concatenate([re.astype(bf16), im.astype(bf16)], axis=1) for re, im in fields], axis=0
    )
    mid = dot(packed, right).astype(bf16)
    turned = jnp.concatenate(
        [
            jnp.concatenate(
                [mid[m * length : (m + 1) * length, c * length : (c + 1) * length] for m in range(len(fields))],
                axis=1,
            )
            for c in range(2)
        ],
        axis=0,
    )
    return split(dot(left, turned), length)


def mul(a, b):
    return (a[0] * b[0] - a[1] * b[1], a[0] * b[1] + a[1] * b[0])


def conj_mul(a, b):
    return (a[0] * b[0] + a[1] * b[1], a[0] * b[1] - a[1] * b[0])


def total(pairs):
    return (sum(p[0] for p in pairs[1:]) + pairs[0][0], sum(p[1] for p in pairs[1:]) + pairs[0][1])


def position_terms(front, rear, probes, observed, tables, prop):
    length = observed.shape[0]
    ahead, behind = tables
    forward = lambda f: transform(f, ahead, behind, length)
    inverse = lambda f: transform(f, behind, ahead, length)
    spec = forward([mul(p, front) for p in probes])
    inner = inverse([mul(s, prop) for s in spec])
    far = forward([mul(s, rear) for s in inner])
    intensity = sum(re * re + im * im for re, im in far[1:]) + far[0][0] ** 2 + far[0][1] ** 2
    factor = 1.0 - jnp.sqrt(observed) / jnp.sqrt(intensity + 1.0)
    back_b = inverse([(re * factor, im * factor) for re, im in far])
    back_spec = forward([conj_mul(rear, b) for b in back_b])
    back_a = inverse([conj_mul(prop, b) for b in back_spec])
    grad_a = total([conj_mul(p, b) for p, b in zip(probes, back_a)])
    grad_b = total([conj_mul(s, b) for s, b in zip(inner, back_b)])
    return grad_a, grad_b, [conj_mul(front, b) for b in back_a]


def position_kernel(n_tile, n_mode, slots, tile_ref, arrived_ref, probe_ref, meas_ref, table_ref, prop_ref, back_ref, pgrad_ref):
    per_dev = meas_ref.shape[0]
    modes = probe_ref.shape[1]
    owner = lax.axis_index("tile") * n_mode + lax.axis_index("mode")
    tiles, order = ranks(tile_ref, owner * per_dev, per_dev)
    tables = (table_ref[0], table_ref[1])
    back_ref[...] = jnp.zeros_like(back_ref)
    for q in range(per_dev):
        place = [(tiles[q] * n_mode + k * n_mode // 2) * slots + order[q] for k in range(2)]
        pair = lambda k: (arrived_ref[place[k], 0].astype(f32), arrived_ref[place[k], 1].astype(f32))
        probes = [(probe_ref[0, m], probe_ref[1, m]) for m in range(modes)]
        grad_a, grad_b, terms = position_terms(
            pair(0), pair(1), probes, meas_ref[q], tables, (prop_ref[0], prop_ref[1])
        )
        for k, grad in enumerate((grad_a, grad_b)):
            for part in range(2):
                back_ref[place[k], part] = grad[part].astype(bf16)
        for m, term in enumerate(terms):
            for part in range(2):
                if q == 0:
                    pgrad_ref[part, m] = term[part]
                else:
                    pgrad_ref[part, m] += term[part]


smem = pl.BlockSpec(memory_space=pltpu.SMEM)
vmem = pl.BlockSpec(memory_space=pltpu.VMEM)
params = pltpu.CompilerParams(vmem_limit_bytes=vmem_bytes)


def communicating(number):
    return pltpu.CompilerParams(
        vmem_limit_bytes=vmem_bytes, collective_id=number, has_side_effects=True
    )


def on_device(object_field, probe_modes, measured, pos_tile, off_row, off_col):
    length = probe_modes.shape[-1]
    margin = length // 2
    tile_rows = object_field.shape[2]
    tile_cols = object_field.shape[3]
    per_dev = measured.shape[1]
    n_tile = lax.axis_size("tile")
    n_mode = lax.axis_size("mode")
    slots = max(2, 2 * per_dev // n_tile)
    owners = n_tile * n_mode
    count = owners * slots
    tables, prop = make_tables(length)
    places = (pos_tile[0, :, 0], off_row[0], off_col[0])
    n_strip = lax.axis_size("strip")
    sizes = (per_dev, slots, n_tile, n_mode, n_strip, margin)
    windows = jax.ShapeDtypeStruct((count, 2, length, length), bf16)
    rows, width = tile_rows + 2 * margin, tile_cols + 2 * length
    dma = pltpu.SemaphoreType.DMA
    arrived = pl.pallas_call(
        lambda *refs: forward_kernel(*sizes, *refs),
        out_shape=windows,
        in_specs=[smem] * 3 + [vmem],
        out_specs=vmem,
        scratch_shapes=[
            pltpu.VMEM((2, rows, width), bf16),
            pltpu.VMEM(windows.shape, bf16),
            *[dma((len(directions),))] * 2,
            *[dma((owners,))] * 2,
        ],
        compiler_params=communicating(0),
        name="forward",
    )(*places, object_field[:, 0])
    back, probe_part = pl.pallas_call(
        lambda *refs: position_kernel(n_tile, n_mode, slots, *refs),
        out_shape=(windows, jax.ShapeDtypeStruct(probe_modes.shape, f32)),
        in_specs=[smem] + [vmem] * 5,
        out_specs=(vmem, vmem),
        compiler_params=params,
        name="positions",
    )(places[0], arrived, probe_modes, measured[0], tables, prop)
    flat = probe_part.reshape(-1, length)
    piece = flat.shape[0] // owners
    object_grad, probe_grad = pl.pallas_call(
        lambda *refs: backward_kernel(*sizes, *refs),
        out_shape=(
            jax.ShapeDtypeStruct((2, tile_rows, tile_cols), f32),
            jax.ShapeDtypeStruct(flat.shape, f32),
        ),
        in_specs=[smem] * 3 + [vmem] * 2,
        out_specs=(vmem, vmem),
        scratch_shapes=[
            pltpu.VMEM(windows.shape, bf16),
            pltpu.VMEM((2, rows, width), f32),
            pltpu.VMEM((2, rows, count * length), bf16),
            pltpu.VMEM((count * length, width), bf16),
            pltpu.VMEM((n_mode, n_tile * piece, length), f32),
            pltpu.VMEM((n_tile * piece, length), f32),
            pltpu.VMEM((n_tile, piece, length), f32),
            pltpu.VMEM((piece, length), f32),
            pltpu.VMEM((n_strip, piece, length), f32),
            *[pltpu.VMEM((2, rows, width), bf16)] * 2,
            *[dma((owners,))] * 2,
            *[dma((n_mode,))] * 2,
            *[dma((n_tile,))] * 2,
            *[dma((n_strip,))] * 2,
            *[dma((n_tile,))] * 2,
            *[dma((n_mode,))] * 2,
            *[dma((len(directions),))] * 2,
        ],
        compiler_params=communicating(1),
        name="backward",
    )(*places, back, flat)
    return (object_grad[:, None], probe_grad.reshape(probe_modes.shape))


def solution(mesh):
    return jax.shard_map(
        on_device,
        mesh=mesh,
        in_specs=(
            P("group", "mode", "strip", "tile"),
            P("group", None, None, None),
            P(("group", "strip"), ("tile", "mode"), None, None),
            P(("group", "strip"), None, None),
            P(("group", "strip"), None),
            P(("group", "strip"), None),
        ),
        out_specs=(P("group", "mode", "strip", "tile"), P("group", None, None, None)),
        check_vma=False,
    )
```

```python
import jax
import jax.numpy as jnp
import numpy as np
from jax import lax
from jax.experimental import pallas as pl
from jax.experimental.pallas import tpu as pltpu
from jax.sharding import PartitionSpec as P

prop_phase = 60.0
vmem_bytes = 48 * 1024 * 1024
f32 = jnp.float32
bf16 = jnp.bfloat16


def make_tables(length):
    indices = np.arange(length)
    angles = (indices[:, None] * indices[None, :] % length) * (2.0 * np.pi / length)
    cos = (np.cos(angles) / np.sqrt(length)).astype(np.float32)
    sin = (-np.sin(angles) / np.sqrt(length)).astype(np.float32)
    forward = np.block([[cos, sin], [-sin, cos]])
    inverse = np.block([[cos, -sin], [sin, cos]])
    shifted = (indices + length // 2) % length - length // 2
    frequency = shifted / length
    phases = -prop_phase * (frequency[:, None] ** 2 + frequency[None, :] ** 2)
    return (
        jnp.asarray(np.stack([forward, inverse])).astype(bf16),
        jnp.asarray(np.stack([np.cos(phases), np.sin(phases)]).astype(np.float32)),
    )


def ranks(tile_ref, first, per_dev):
    tiles = [tile_ref[first + q] for q in range(per_dev)]
    out = []
    for q in range(per_dev):
        rank = jnp.int32(0)
        for earlier in range(q):
            rank = rank + jnp.where(tiles[earlier] == tiles[q], 1, 0)
        out.append(rank)
    return tiles, out


def slot_place(refs, owner, slot, tile, per_dev):
    tile_ref, row_ref, col_ref = refs
    first = owner * per_dev
    tiles, order = ranks(tile_ref, first, per_dev)
    row, col, keep = jnp.int32(0), jnp.int32(0), jnp.int32(0)
    for q in range(per_dev):
        hit = jnp.where((tiles[q] == tile) & (order[q] == slot), 1, 0)
        row = row + hit * row_ref[first + q]
        col = col + hit * col_ref[first + q]
        keep = keep + hit
    return row, col, keep


def one_hot(shape, dim, shift, keep=None):
    wide = lax.broadcasted_iota(jnp.int32, shape, dim)
    narrow = lax.broadcasted_iota(jnp.int32, shape, 1 - dim)
    hit = wide == narrow + shift
    if keep is not None:
        hit = hit & (keep > 0)
    return jnp.where(hit, 1.0, 0.0).astype(bf16)


def dot(a, b):
    return jnp.dot(a, b, preferred_element_type=f32)


def remote(src, dst, send, recv, device):
    return pltpu.make_async_remote_copy(
        src_ref=src,
        dst_ref=dst,
        send_sem=send,
        recv_sem=recv,
        device_id=device,
        device_id_type=pl.DeviceIdType.MESH,
    )


def owner_id(owner, n_mode):
    return {"tile": owner // n_mode, "mode": owner % n_mode}


def others(me, count, act, start=None):
    first = count // 2 if start is None else start

    def body(step, carry):
        other = lax.rem(me + first + step, count)

        @pl.when(other != me)
        def _():
            act(other)

        return carry

    lax.fori_loop(0, count, body, 0)


directions = [(dt, ds) for ds in (-1, 0, 1) for dt in (-1, 0, 1) if (dt, ds) != (0, 0)]


def exists(here, count, step):
    if step == 0:
        return jnp.int32(1)
    return jnp.minimum(count - 1 - here if step > 0 else here, 1)


def neighbour(spot, direction, sign):
    tile, strip, n_tile, n_strip = spot
    dt, ds = (sign * d for d in direction)
    there = exists(tile, n_tile, dt) * exists(strip, n_strip, ds)
    return there, {"tile": tile + dt, "strip": strip + ds}


def greet(me, owners, n_mode, spot):
    barrier = pltpu.get_barrier_semaphore()
    tile, strip, n_tile, n_strip = spot

    def call(device):
        pl.semaphore_signal(barrier, inc=1, device_id=device, device_id_type=pl.DeviceIdType.MESH)

    others(me, owners, lambda other: call(owner_id(other, n_mode)))
    others(strip, n_strip, lambda other: call({"strip": other}))
    amount = owners + n_strip - 2
    for direction in directions:
        if 0 not in direction:
            there, device = neighbour(spot, direction, 1)
            pl.when(there > 0)(lambda: call(device))
            amount = amount + there
    pl.semaphore_wait(barrier, amount)


def side(step, before, middle, after):
    return ((0, before), (before, middle), (before + middle, after))[step + 1]


def margin_part(ref, dt, ds, tile_rows, tile_cols, margin, length):
    row, row_count = side(ds, margin, tile_rows, margin)
    col, col_count = side(dt, length, tile_cols, length)
    return ref.at[:, pl.ds(row, row_count), pl.ds(col, col_count)]


def forward_kernel(
    per_dev, slots, n_tile, n_mode, n_strip, margin,
    tile_ref, row_ref, col_ref, object_ref, arrived_ref,
    padded_ref, out_ref, halo_send, halo_recv, send_sem, recv_sem,
):
    tile, mode, strip = (lax.axis_index(axis) for axis in ("tile", "mode", "strip"))
    me, owners = tile * n_mode + mode, n_tile * n_mode
    length = out_ref.shape[-1]
    _, tile_rows, tile_cols = object_ref.shape
    _, rows, width = padded_ref.shape
    spot = (tile, strip, n_tile, n_strip)
    greet(me, owners, n_mode, spot)

    def edge(dt, ds):
        row = {1: tile_rows - margin}.get(ds, 0)
        col = {1: tile_cols - length}.get(dt, 0)
        return object_ref.at[
            :, pl.ds(row, margin if ds else tile_rows), pl.ds(col, length if dt else tile_cols)
        ]

    def region(dt, ds):
        return margin_part(padded_ref, dt, ds, tile_rows, tile_cols, margin, length)

    def halo(number, sign):
        dt, ds = directions[number]
        there, device = neighbour(spot, (dt, ds), sign)
        copy = remote(edge(dt, ds), region(-dt, -ds), halo_send.at[number], halo_recv.at[number], device)
        return there, copy

    for number in range(len(directions)):
        there, copy = halo(number, 1)
        pl.when(there > 0)(copy.start)
    region(0, 0)[...] = object_ref[...]
    for number, (dt, ds) in enumerate(directions):
        there, _ = neighbour(spot, (dt, ds), -1)
        target = region(-dt, -ds)

        @pl.when(there == 0)
        def _():
            target[...] = jnp.zeros(target.shape, bf16)

    for number in range(len(directions)):
        there, copy = halo(number, 1)
        pl.when(there > 0)(copy.wait_send)
        there, copy = halo(number, -1)
        pl.when(there > 0)(copy.wait_recv)

    def span(owner):
        return pl.ds(owner * slots, slots)

    def body(step, carry):
        owner = lax.rem(me + owners // 2 + step, owners)
        for slot in range(slots):
            row, col, _ = slot_place((tile_ref, row_ref, col_ref), owner, slot, tile, per_dev)
            col = col + margin
            pick_row = one_hot((length, rows), 1, row)
            outer = 2 * length
            pick_col = one_hot((2 * outer, length), 0, jnp.where(col < outer, col, col - width + 2 * outer))
            for part in range(2):
                strips = [
                    dot(pick_row, padded_ref[part, :, pl.ds(at, outer)]).astype(bf16)
                    for at in (0, width - outer)
                ]
                window = dot(jnp.concatenate(strips, axis=1), pick_col)
                out_ref[owner * slots + slot, part] = window.astype(bf16)

        @pl.when(owner != me)
        def _():
            remote(
                out_ref.at[span(owner)], arrived_ref.at[span(me)],
                send_sem.at[owner], recv_sem.at[me], owner_id(owner, n_mode),
            ).start()

        return carry

    lax.fori_loop(0, owners, body, 0)
    arrived_ref[span(me)] = out_ref[span(me)]

    def finish(other):
        copy = remote(
            out_ref.at[span(other)], arrived_ref.at[span(other)],
            send_sem.at[other], recv_sem.at[other], owner_id(other, n_mode),
        )
        copy.wait_send()
        copy.wait_recv()

    others(me, owners, finish)


def backward_kernel(
    per_dev, slots, n_tile, n_mode, n_strip, margin,
    tile_ref, row_ref, col_ref, back_ref, part_ref, object_ref, probe_ref,
    returned_ref, grid_ref, spread_ref, put_ref, pair_ref, half_ref, rs_ref, sum_ref, strip_ref,
    margin_out, margin_in,
    send_sem, recv_sem, pair_send, pair_recv, rs_send, rs_recv, st_send, st_recv,
    ag_send, ag_recv, join_send, join_recv, margin_send, margin_recv,
):
    tile, mode, strip = (lax.axis_index(axis) for axis in ("tile", "mode", "strip"))
    me, owners = tile * n_mode + mode, n_tile * n_mode
    count = owners * slots
    length = back_ref.shape[-1]
    _, tile_rows, tile_cols = object_ref.shape
    _, rows, width = grid_ref.shape
    piece = rs_ref.shape[1]
    half = n_tile * piece
    spot = (tile, strip, n_tile, n_strip)
    greet(me, owners, n_mode, spot)

    def span(owner):
        return pl.ds(owner * slots, slots)

    def share(index, size):
        return pl.ds(pl.multiple_of(index * size, piece), size)

    def pair_copy(other, source):
        return remote(
            part_ref.at[share(other, half)], pair_ref.at[source],
            pair_send.at[other], pair_recv.at[source], {"mode": other},
        )

    def reduce_copy(other, source):
        return remote(
            half_ref.at[share(other, piece)], rs_ref.at[source],
            rs_send.at[other], rs_recv.at[source], {"tile": other},
        )

    def window_copy(other, source):
        return remote(
            back_ref.at[span(other)], returned_ref.at[span(source)],
            send_sem.at[other], recv_sem.at[source], owner_id(other, n_mode),
        )

    def strip_copy(other, source):
        return remote(
            sum_ref, strip_ref.at[source], st_send.at[other], st_recv.at[source], {"strip": other}
        )

    def gather_copy(other, source):
        return remote(
            probe_ref.at[share(mode * n_tile + tile, piece)],
            probe_ref.at[share(mode * n_tile + source, piece)],
            ag_send.at[other], ag_recv.at[source], {"tile": other},
        )

    def join_copy(other, source):
        return remote(
            probe_ref.at[share(mode, half)], probe_ref.at[share(source, half)],
            join_send.at[other], join_recv.at[source], {"mode": other},
        )

    def finish(make):
        def act(other):
            make(other, other).wait_send()
            make(other, other).wait_recv()

        return act

    others(mode, n_mode, lambda other: pair_copy(other, mode).start())
    others(me, owners, lambda other: window_copy(other, me).start())
    pair_ref[mode] = part_ref[share(mode, half)]
    returned_ref[span(me)] = back_ref[span(me)]
    others(mode, n_mode, finish(pair_copy))
    half_ref[...] = lax.fori_loop(1, n_mode, lambda i, acc: acc + pair_ref[i], pair_ref[0])
    others(tile, n_tile, lambda other: reduce_copy(other, tile).start())
    rs_ref[tile] = half_ref[share(tile, piece)]
    refs = (tile_ref, row_ref, col_ref)

    def sender(step):
        return lax.rem(me + 2 * owners - owners // 2 - step, owners)

    def build(index, carry):
        _, col, _ = slot_place(refs, sender(index // slots), index % slots, tile, per_dev)
        where = pl.ds(pl.multiple_of(index * length, length), length)
        put_ref[where, :] = one_hot((length, width), 1, col + margin)
        return carry

    lax.fori_loop(0, count, build, 0)
    others(tile, n_tile, finish(reduce_copy))
    sum_ref[...] = lax.fori_loop(1, n_tile, lambda i, acc: acc + rs_ref[i], rs_ref[0])
    others(strip, n_strip, lambda other: strip_copy(other, strip).start())
    strip_ref[strip] = sum_ref[...]
    others(strip, n_strip, finish(strip_copy))
    probe_ref[share(mode * n_tile + tile, piece)] = lax.fori_loop(
        1, n_strip, lambda i, acc: acc + strip_ref[i], strip_ref[0]
    )
    others(tile, n_tile, lambda other: gather_copy(other, tile).start())

    def place(step, carry):
        owner = sender(step)

        @pl.when(owner != me)
        def _():
            finish(window_copy)(owner)

        for slot in range(slots):
            row, _, keep = slot_place(refs, owner, slot, tile, per_dev)
            where = pl.ds(pl.multiple_of((step * slots + slot) * length, length), length)
            put_row = one_hot((rows, length), 0, row, keep)
            for part in range(2):
                spread_ref[part, :, where] = dot(put_row, returned_ref[owner * slots + slot, part]).astype(bf16)
        return carry

    outer = 2 * length
    grid_ref[:, :, pl.ds(outer, width - 2 * outer)] = jnp.zeros((2, rows, width - 2 * outer), f32)

    def fill(first, last, add):
        depth = pl.ds(first * slots * length, (last - first) * slots * length)
        for col in (0, width - outer):
            where = pl.ds(col, outer)
            for part in range(2):
                product = dot(spread_ref[part, :, depth], put_ref[depth, where])
                grid_ref[part, :, where] = grid_ref[part, :, where] + product if add else product

    early = 3 * owners // 4
    lax.fori_loop(0, early, place, 0)
    fill(0, early, False)
    lax.fori_loop(early, owners, place, 0)
    fill(early, owners, True)

    def region(ref, dt, ds):
        return margin_part(ref, dt, ds, tile_rows, tile_cols, margin, length)

    def margin_copy(number, sign):
        dt, ds = directions[number]
        there, device = neighbour(spot, (dt, ds), sign)
        copy = remote(
            region(margin_out, dt, ds), region(margin_in, -dt, -ds),
            margin_send.at[number], margin_recv.at[number], device,
        )
        return there, copy

    def send_margins(columns):
        for number, (dt, ds) in enumerate(directions):
            if (dt != 0) == columns:
                region(margin_out, dt, ds)[...] = region(grid_ref, dt, ds)[...].astype(bf16)
                there, copy = margin_copy(number, 1)
                pl.when(there > 0)(copy.start)

    send_margins(True)
    send_margins(False)
    others(tile, n_tile, finish(gather_copy))
    others(mode, n_mode, lambda other: join_copy(other, mode).start())
    object_ref[...] = region(grid_ref, 0, 0)[...]
    for number, (dt, ds) in enumerate(directions):
        there, copy = margin_copy(number, 1)
        pl.when(there > 0)(copy.wait_send)
        there, copy = margin_copy(number, -1)
        row = {-1: tile_rows - margin}.get(ds, 0)
        col = {-1: tile_cols - length}.get(dt, 0)
        target = object_ref.at[
            :, pl.ds(row, margin if ds else tile_rows), pl.ds(col, length if dt else tile_cols)
        ]
        arriving = region(margin_in, -dt, -ds)

        @pl.when(there > 0)
        def _():
            copy.wait_recv()
            target[...] += arriving[...].astype(f32)

    others(mode, n_mode, finish(join_copy))


def split(field, length):
    modes = field.shape[1] // length
    return [
        (field[:length, m * length : (m + 1) * length], field[length:, m * length : (m + 1) * length])
        for m in range(modes)
    ]


def transform(fields, right, left, length):
    packed = jnp.concatenate(
        [jnp.concatenate([re.astype(bf16), im.astype(bf16)], axis=1) for re, im in fields], axis=0
    )
    mid = dot(packed, right).astype(bf16)
    turned = jnp.concatenate(
        [
            jnp.concatenate(
                [mid[m * length : (m + 1) * length, c * length : (c + 1) * length] for m in range(len(fields))],
                axis=1,
            )
            for c in range(2)
        ],
        axis=0,
    )
    return split(dot(left, turned), length)


def mul(a, b):
    return (a[0] * b[0] - a[1] * b[1], a[0] * b[1] + a[1] * b[0])


def conj_mul(a, b):
    return (a[0] * b[0] + a[1] * b[1], a[0] * b[1] - a[1] * b[0])


def total(pairs):
    return (sum(p[0] for p in pairs[1:]) + pairs[0][0], sum(p[1] for p in pairs[1:]) + pairs[0][1])


def position_terms(fronts, rears, probes, observed, tables, prop):
    length = observed[0].shape[0]
    modes = len(probes)
    ahead, behind = tables
    forward = lambda f: transform(f, ahead, behind, length)
    inverse = lambda f: transform(f, behind, ahead, length)
    each = range(len(fronts) * modes)
    front = lambda i: fronts[i // modes]()
    rear = lambda i: rears[i // modes]()
    probe = lambda i: probes[i % modes]
    spec = forward([mul(probe(i), front(i)) for i in each])
    inner = inverse([mul(s, prop) for s in spec])
    far = forward([mul(inner[i], rear(i)) for i in each])
    resid = []
    for q, seen in enumerate(observed):
        mine = far[q * modes : (q + 1) * modes]
        intensity = sum(re * re + im * im for re, im in mine[1:]) + mine[0][0] ** 2 + mine[0][1] ** 2
        factor = 1.0 - jnp.sqrt(seen) / jnp.sqrt(intensity + 1.0)
        resid += [(re * factor, im * factor) for re, im in mine]
    back_b = inverse(resid)
    back_spec = forward([conj_mul(rear(i), back_b[i]) for i in each])
    back_a = inverse([conj_mul(prop, b) for b in back_spec])
    grads = []
    for q in range(len(fronts)):
        mine = range(q * modes, (q + 1) * modes)
        grads.append(
            (
                total([conj_mul(probe(i), back_a[i]) for i in mine]),
                total([conj_mul(inner[i], back_b[i]) for i in mine]),
            )
        )
    terms = [
        total([conj_mul(fronts[q](), back_a[q * modes + m]) for q in range(len(fronts))])
        for m in range(modes)
    ]
    return grads, terms


def position_kernel(n_tile, n_mode, slots, tile_ref, arrived_ref, probe_ref, meas_ref, table_ref, prop_ref, back_ref, pgrad_ref):
    per_dev = meas_ref.shape[0]
    modes = probe_ref.shape[1]
    owner = lax.axis_index("tile") * n_mode + lax.axis_index("mode")
    tiles, order = ranks(tile_ref, owner * per_dev, per_dev)
    back_ref[...] = jnp.zeros_like(back_ref)
    place = [
        [(tiles[q] * n_mode + k * n_mode // 2) * slots + order[q] for k in range(2)]
        for q in range(per_dev)
    ]

    def window(q, k):
        return lambda: tuple(arrived_ref[place[q][k], part].astype(f32) for part in range(2))

    grads, terms = position_terms(
        [window(q, 0) for q in range(per_dev)],
        [window(q, 1) for q in range(per_dev)],
        [(probe_ref[0, m], probe_ref[1, m]) for m in range(modes)],
        [meas_ref[q] for q in range(per_dev)],
        (table_ref[0], table_ref[1]),
        (prop_ref[0], prop_ref[1]),
    )
    for q in range(per_dev):
        for k in range(2):
            for part in range(2):
                back_ref[place[q][k], part] = grads[q][k][part].astype(bf16)
    for m in range(modes):
        for part in range(2):
            pgrad_ref[part, m] = terms[m][part]


smem = pl.BlockSpec(memory_space=pltpu.SMEM)
vmem = pl.BlockSpec(memory_space=pltpu.VMEM)
params = pltpu.CompilerParams(vmem_limit_bytes=vmem_bytes)


def communicating(number):
    return pltpu.CompilerParams(
        vmem_limit_bytes=vmem_bytes, collective_id=number, has_side_effects=True
    )


def on_device(object_field, probe_modes, measured, pos_tile, off_row, off_col):
    length = probe_modes.shape[-1]
    margin = length // 2
    tile_rows = object_field.shape[2]
    tile_cols = object_field.shape[3]
    per_dev = measured.shape[1]
    n_tile = lax.axis_size("tile")
    n_mode = lax.axis_size("mode")
    slots = max(2, 2 * per_dev // n_tile)
    owners = n_tile * n_mode
    count = owners * slots
    tables, prop = make_tables(length)
    places = (pos_tile[0, :, 0], off_row[0], off_col[0])
    n_strip = lax.axis_size("strip")
    sizes = (per_dev, slots, n_tile, n_mode, n_strip, margin)
    windows = jax.ShapeDtypeStruct((count, 2, length, length), bf16)
    rows, width = tile_rows + 2 * margin, tile_cols + 2 * length
    dma = pltpu.SemaphoreType.DMA
    arrived = pl.pallas_call(
        lambda *refs: forward_kernel(*sizes, *refs),
        out_shape=windows,
        in_specs=[smem] * 3 + [vmem],
        out_specs=vmem,
        scratch_shapes=[
            pltpu.VMEM((2, rows, width), bf16),
            pltpu.VMEM(windows.shape, bf16),
            *[dma((len(directions),))] * 2,
            *[dma((owners,))] * 2,
        ],
        compiler_params=communicating(0),
        name="forward",
    )(*places, object_field[:, 0])
    back, probe_part = pl.pallas_call(
        lambda *refs: position_kernel(n_tile, n_mode, slots, *refs),
        out_shape=(windows, jax.ShapeDtypeStruct(probe_modes.shape, f32)),
        in_specs=[smem] + [vmem] * 5,
        out_specs=(vmem, vmem),
        compiler_params=params,
        name="positions",
    )(places[0], arrived, probe_modes, measured[0], tables, prop)
    flat = probe_part.reshape(-1, length)
    piece = flat.shape[0] // owners
    object_grad, probe_grad = pl.pallas_call(
        lambda *refs: backward_kernel(*sizes, *refs),
        out_shape=(
            jax.ShapeDtypeStruct((2, tile_rows, tile_cols), f32),
            jax.ShapeDtypeStruct(flat.shape, f32),
        ),
        in_specs=[smem] * 3 + [vmem] * 2,
        out_specs=(vmem, vmem),
        scratch_shapes=[
            pltpu.VMEM(windows.shape, bf16),
            pltpu.VMEM((2, rows, width), f32),
            pltpu.VMEM((2, rows, count * length), bf16),
            pltpu.VMEM((count * length, width), bf16),
            pltpu.VMEM((n_mode, n_tile * piece, length), f32),
            pltpu.VMEM((n_tile * piece, length), f32),
            pltpu.VMEM((n_tile, piece, length), f32),
            pltpu.VMEM((piece, length), f32),
            pltpu.VMEM((n_strip, piece, length), f32),
            *[pltpu.VMEM((2, rows, width), bf16)] * 2,
            *[dma((owners,))] * 2,
            *[dma((n_mode,))] * 2,
            *[dma((n_tile,))] * 2,
            *[dma((n_strip,))] * 2,
            *[dma((n_tile,))] * 2,
            *[dma((n_mode,))] * 2,
            *[dma((len(directions),))] * 2,
        ],
        compiler_params=communicating(1),
        name="backward",
    )(*places, back, flat)
    return (object_grad[:, None], probe_grad.reshape(probe_modes.shape))


def solution(mesh):
    return jax.shard_map(
        on_device,
        mesh=mesh,
        in_specs=(
            P("group", "mode", "strip", "tile"),
            P("group", None, None, None),
            P(("group", "strip"), ("tile", "mode"), None, None),
            P(("group", "strip"), None, None),
            P(("group", "strip"), None),
            P(("group", "strip"), None),
        ),
        out_specs=(P("group", "mode", "strip", "tile"), P("group", None, None, None)),
        check_vma=False,
    )
```

```python
import jax
import jax.numpy as jnp
import numpy as np
from jax import lax
from jax.experimental import pallas as pl
from jax.experimental.pallas import tpu as pltpu
from jax.sharding import PartitionSpec as P

prop_phase = 60.0
vmem_bytes = 48 * 1024 * 1024
f32 = jnp.float32
bf16 = jnp.bfloat16


def make_tables(length):
    indices = np.arange(length)
    angles = (indices[:, None] * indices[None, :] % length) * (2.0 * np.pi / length)
    cos = (np.cos(angles) / np.sqrt(length)).astype(np.float32)
    sin = (-np.sin(angles) / np.sqrt(length)).astype(np.float32)
    forward = np.block([[cos, sin], [-sin, cos]])
    inverse = np.block([[cos, -sin], [sin, cos]])
    shifted = (indices + length // 2) % length - length // 2
    frequency = shifted / length
    phases = -prop_phase * (frequency[:, None] ** 2 + frequency[None, :] ** 2)
    return (
        jnp.asarray(np.stack([forward, inverse])).astype(bf16),
        jnp.asarray(np.stack([np.cos(phases), np.sin(phases)]).astype(np.float32)),
    )


def ranks(tile_ref, first, per_dev):
    tiles = [tile_ref[first + q] for q in range(per_dev)]
    out = []
    for q in range(per_dev):
        rank = jnp.int32(0)
        for earlier in range(q):
            rank = rank + jnp.where(tiles[earlier] == tiles[q], 1, 0)
        out.append(rank)
    return tiles, out


def slot_place(refs, owner, slot, tile, per_dev):
    tile_ref, row_ref, col_ref = refs
    first = owner * per_dev
    tiles, order = ranks(tile_ref, first, per_dev)
    row, col, keep = jnp.int32(0), jnp.int32(0), jnp.int32(0)
    for q in range(per_dev):
        hit = jnp.where((tiles[q] == tile) & (order[q] == slot), 1, 0)
        row = row + hit * row_ref[first + q]
        col = col + hit * col_ref[first + q]
        keep = keep + hit
    return row, col, keep


def one_hot(shape, dim, shift, keep=None):
    wide = lax.broadcasted_iota(jnp.int32, shape, dim)
    narrow = lax.broadcasted_iota(jnp.int32, shape, 1 - dim)
    hit = wide == narrow + shift
    if keep is not None:
        hit = hit & (keep > 0)
    return jnp.where(hit, 1.0, 0.0).astype(bf16)


def dot(a, b):
    return jnp.dot(a, b, preferred_element_type=f32)


def remote(src, dst, send, recv, device):
    return pltpu.make_async_remote_copy(
        src_ref=src,
        dst_ref=dst,
        send_sem=send,
        recv_sem=recv,
        device_id=device,
        device_id_type=pl.DeviceIdType.MESH,
    )


def owner_id(owner, n_mode):
    return {"tile": owner // n_mode, "mode": owner % n_mode}


def others(me, count, act, start=None):
    first = count // 2 if start is None else start

    def body(step, carry):
        other = lax.rem(me + first + step, count)

        @pl.when(other != me)
        def _():
            act(other)

        return carry

    lax.fori_loop(0, count, body, 0)


directions = [(dt, ds) for ds in (-1, 0, 1) for dt in (-1, 0, 1) if (dt, ds) != (0, 0)]


def exists(here, count, step):
    if step == 0:
        return jnp.int32(1)
    return jnp.minimum(count - 1 - here if step > 0 else here, 1)


def neighbour(spot, direction, sign):
    tile, strip, n_tile, n_strip = spot
    dt, ds = (sign * d for d in direction)
    there = exists(tile, n_tile, dt) * exists(strip, n_strip, ds)
    return there, {"tile": tile + dt, "strip": strip + ds}


def greet(me, owners, n_mode, spot):
    barrier = pltpu.get_barrier_semaphore()
    tile, strip, n_tile, n_strip = spot

    def call(device):
        pl.semaphore_signal(barrier, inc=1, device_id=device, device_id_type=pl.DeviceIdType.MESH)

    others(me, owners, lambda other: call(owner_id(other, n_mode)))
    others(strip, n_strip, lambda other: call({"strip": other}))
    amount = owners + n_strip - 2
    for direction in directions:
        if 0 not in direction:
            there, device = neighbour(spot, direction, 1)
            pl.when(there > 0)(lambda: call(device))
            amount = amount + there
    pl.semaphore_wait(barrier, amount)


def side(step, before, middle, after):
    return ((0, before), (before, middle), (before + middle, after))[step + 1]


def margin_part(ref, dt, ds, tile_rows, tile_cols, margin, length):
    row, row_count = side(ds, margin, tile_rows, margin)
    col, col_count = side(dt, length, tile_cols, length)
    return ref.at[:, pl.ds(row, row_count), pl.ds(col, col_count)]


def forward_kernel(
    per_dev, slots, n_tile, n_mode, n_strip, margin,
    tile_ref, row_ref, col_ref, object_ref, arrived_ref,
    padded_ref, out_ref, halo_send, halo_recv, send_sem, recv_sem,
):
    tile, mode, strip = (lax.axis_index(axis) for axis in ("tile", "mode", "strip"))
    me, owners = tile * n_mode + mode, n_tile * n_mode
    length = out_ref.shape[-1]
    _, tile_rows, tile_cols = object_ref.shape
    _, rows, width = padded_ref.shape
    spot = (tile, strip, n_tile, n_strip)
    greet(me, owners, n_mode, spot)

    def edge(dt, ds):
        row = {1: tile_rows - margin}.get(ds, 0)
        col = {1: tile_cols - length}.get(dt, 0)
        return object_ref.at[
            :, pl.ds(row, margin if ds else tile_rows), pl.ds(col, length if dt else tile_cols)
        ]

    def region(dt, ds):
        return margin_part(padded_ref, dt, ds, tile_rows, tile_cols, margin, length)

    def halo(number, sign):
        dt, ds = directions[number]
        there, device = neighbour(spot, (dt, ds), sign)
        copy = remote(edge(dt, ds), region(-dt, -ds), halo_send.at[number], halo_recv.at[number], device)
        return there, copy

    for number in range(len(directions)):
        there, copy = halo(number, 1)
        pl.when(there > 0)(copy.start)
    region(0, 0)[...] = object_ref[...]
    for number, (dt, ds) in enumerate(directions):
        there, _ = neighbour(spot, (dt, ds), -1)
        target = region(-dt, -ds)

        @pl.when(there == 0)
        def _():
            target[...] = jnp.zeros(target.shape, bf16)

    for number in range(len(directions)):
        there, copy = halo(number, 1)
        pl.when(there > 0)(copy.wait_send)
        there, copy = halo(number, -1)
        pl.when(there > 0)(copy.wait_recv)

    def span(owner):
        return pl.ds(owner * slots, slots)

    def body(step, carry):
        owner = lax.rem(me + owners // 2 + step, owners)
        for slot in range(slots):
            row, col, _ = slot_place((tile_ref, row_ref, col_ref), owner, slot, tile, per_dev)
            col = col + margin
            pick_row = one_hot((length, rows), 1, row)
            outer = 2 * length
            pick_col = one_hot((2 * outer, length), 0, jnp.where(col < outer, col, col - width + 2 * outer))
            for part in range(2):
                strips = [
                    dot(pick_row, padded_ref[part, :, pl.ds(at, outer)]).astype(bf16)
                    for at in (0, width - outer)
                ]
                window = dot(jnp.concatenate(strips, axis=1), pick_col)
                out_ref[owner * slots + slot, part] = window.astype(bf16)

        @pl.when(owner != me)
        def _():
            remote(
                out_ref.at[span(owner)], arrived_ref.at[span(me)],
                send_sem.at[owner], recv_sem.at[me], owner_id(owner, n_mode),
            ).start()

        return carry

    lax.fori_loop(0, owners, body, 0)
    arrived_ref[span(me)] = out_ref[span(me)]

    def finish(other):
        copy = remote(
            out_ref.at[span(other)], arrived_ref.at[span(other)],
            send_sem.at[other], recv_sem.at[other], owner_id(other, n_mode),
        )
        copy.wait_send()
        copy.wait_recv()

    others(me, owners, finish)


def backward_kernel(
    per_dev, slots, n_tile, n_mode, n_strip, margin,
    tile_ref, row_ref, col_ref, back_ref, part_ref, object_ref, probe_ref,
    returned_ref, grid_ref, spread_ref, put_ref, pair_ref, half_ref, rs_ref, sum_ref, strip_ref,
    margin_out, margin_in,
    send_sem, recv_sem, pair_send, pair_recv, rs_send, rs_recv, st_send, st_recv,
    ag_send, ag_recv, join_send, join_recv, margin_send, margin_recv,
):
    tile, mode, strip = (lax.axis_index(axis) for axis in ("tile", "mode", "strip"))
    me, owners = tile * n_mode + mode, n_tile * n_mode
    count = owners * slots
    length = back_ref.shape[-1]
    _, tile_rows, tile_cols = object_ref.shape
    _, rows, width = grid_ref.shape
    piece = rs_ref.shape[1]
    half = n_tile * piece
    spot = (tile, strip, n_tile, n_strip)
    greet(me, owners, n_mode, spot)

    def span(owner):
        return pl.ds(owner * slots, slots)

    def share(index, size):
        return pl.ds(pl.multiple_of(index * size, piece), size)

    def pair_copy(other, source):
        return remote(
            part_ref.at[share(other, half)], pair_ref.at[source],
            pair_send.at[other], pair_recv.at[source], {"mode": other},
        )

    def reduce_copy(other, source):
        return remote(
            half_ref.at[share(other, piece)], rs_ref.at[source],
            rs_send.at[other], rs_recv.at[source], {"tile": other},
        )

    def window_copy(other, source):
        return remote(
            back_ref.at[span(other)], returned_ref.at[span(source)],
            send_sem.at[other], recv_sem.at[source], owner_id(other, n_mode),
        )

    def strip_copy(other, source):
        return remote(
            sum_ref, strip_ref.at[source], st_send.at[other], st_recv.at[source], {"strip": other}
        )

    def gather_copy(other, source):
        return remote(
            probe_ref.at[share(mode * n_tile + tile, piece)],
            probe_ref.at[share(mode * n_tile + source, piece)],
            ag_send.at[other], ag_recv.at[source], {"tile": other},
        )

    def join_copy(other, source):
        return remote(
            probe_ref.at[share(mode, half)], probe_ref.at[share(source, half)],
            join_send.at[other], join_recv.at[source], {"mode": other},
        )

    def finish(make):
        def act(other):
            make(other, other).wait_send()
            make(other, other).wait_recv()

        return act

    others(mode, n_mode, lambda other: pair_copy(other, mode).start())

    def send_windows(first, last):
        def body(step, carry):
            other = lax.rem(me + owners // 2 + step, owners)

            @pl.when(other != me)
            def _():
                window_copy(other, me).start()

            return carry

        lax.fori_loop(first, last, body, 0)

    send_windows(0, 1)
    pair_ref[mode] = part_ref[share(mode, half)]
    returned_ref[span(me)] = back_ref[span(me)]
    others(mode, n_mode, finish(pair_copy))
    half_ref[...] = lax.fori_loop(1, n_mode, lambda i, acc: acc + pair_ref[i], pair_ref[0])
    others(tile, n_tile, lambda other: reduce_copy(other, tile).start())
    send_windows(1, owners // 2)
    rs_ref[tile] = half_ref[share(tile, piece)]
    refs = (tile_ref, row_ref, col_ref)

    def sender(step):
        return lax.rem(me + 2 * owners - owners // 2 - step, owners)

    def build(index, carry):
        _, col, _ = slot_place(refs, sender(index // slots), index % slots, tile, per_dev)
        where = pl.ds(pl.multiple_of(index * length, length), length)
        put_ref[where, :] = one_hot((length, width), 1, col + margin)
        return carry

    lax.fori_loop(0, count, build, 0)
    others(tile, n_tile, finish(reduce_copy))
    sum_ref[...] = lax.fori_loop(1, n_tile, lambda i, acc: acc + rs_ref[i], rs_ref[0])
    others(strip, n_strip, lambda other: strip_copy(other, strip).start())
    strip_ref[strip] = sum_ref[...]
    others(strip, n_strip, finish(strip_copy))
    probe_ref[share(mode * n_tile + tile, piece)] = lax.fori_loop(
        1, n_strip, lambda i, acc: acc + strip_ref[i], strip_ref[0]
    )
    others(tile, n_tile, lambda other: gather_copy(other, tile).start())
    send_windows(owners // 2, owners)

    def place(step, carry):
        owner = sender(step)

        @pl.when(owner != me)
        def _():
            finish(window_copy)(owner)

        for slot in range(slots):
            row, _, keep = slot_place(refs, owner, slot, tile, per_dev)
            where = pl.ds(pl.multiple_of((step * slots + slot) * length, length), length)
            put_row = one_hot((rows, length), 0, row, keep)
            for part in range(2):
                spread_ref[part, :, where] = dot(put_row, returned_ref[owner * slots + slot, part]).astype(bf16)
        return carry

    outer = 2 * length
    grid_ref[:, :, pl.ds(outer, width - 2 * outer)] = jnp.zeros((2, rows, width - 2 * outer), f32)

    def fill(first, last, add):
        depth = pl.ds(first * slots * length, (last - first) * slots * length)
        for col in (0, width - outer):
            where = pl.ds(col, outer)
            for part in range(2):
                product = dot(spread_ref[part, :, depth], put_ref[depth, where])
                grid_ref[part, :, where] = grid_ref[part, :, where] + product if add else product

    early = 3 * owners // 4
    lax.fori_loop(0, early, place, 0)
    fill(0, early, False)
    lax.fori_loop(early, owners, place, 0)
    fill(early, owners, True)

    def region(ref, dt, ds):
        return margin_part(ref, dt, ds, tile_rows, tile_cols, margin, length)

    def margin_copy(number, sign):
        dt, ds = directions[number]
        there, device = neighbour(spot, (dt, ds), sign)
        copy = remote(
            region(margin_out, dt, ds), region(margin_in, -dt, -ds),
            margin_send.at[number], margin_recv.at[number], device,
        )
        return there, copy

    def send_margins(columns):
        for number, (dt, ds) in enumerate(directions):
            if (dt != 0) == columns:
                region(margin_out, dt, ds)[...] = region(grid_ref, dt, ds)[...].astype(bf16)
                there, copy = margin_copy(number, 1)
                pl.when(there > 0)(copy.start)

    send_margins(True)
    send_margins(False)
    others(tile, n_tile, finish(gather_copy))
    others(mode, n_mode, lambda other: join_copy(other, mode).start())
    object_ref[...] = region(grid_ref, 0, 0)[...]
    for number, (dt, ds) in enumerate(directions):
        there, copy = margin_copy(number, 1)
        pl.when(there > 0)(copy.wait_send)
        there, copy = margin_copy(number, -1)
        row = {-1: tile_rows - margin}.get(ds, 0)
        col = {-1: tile_cols - length}.get(dt, 0)
        target = object_ref.at[
            :, pl.ds(row, margin if ds else tile_rows), pl.ds(col, length if dt else tile_cols)
        ]
        arriving = region(margin_in, -dt, -ds)

        @pl.when(there > 0)
        def _():
            copy.wait_recv()
            target[...] += arriving[...].astype(f32)

    others(mode, n_mode, finish(join_copy))


def split(field, length):
    modes = field.shape[1] // length
    return [
        (field[:length, m * length : (m + 1) * length], field[length:, m * length : (m + 1) * length])
        for m in range(modes)
    ]


def transform(fields, right, left, length):
    packed = jnp.concatenate(
        [jnp.concatenate([re.astype(bf16), im.astype(bf16)], axis=1) for re, im in fields], axis=0
    )
    mid = dot(packed, right).astype(bf16)
    turned = jnp.concatenate(
        [
            jnp.concatenate(
                [mid[m * length : (m + 1) * length, c * length : (c + 1) * length] for m in range(len(fields))],
                axis=1,
            )
            for c in range(2)
        ],
        axis=0,
    )
    return split(dot(left, turned), length)


def mul(a, b):
    return (a[0] * b[0] - a[1] * b[1], a[0] * b[1] + a[1] * b[0])


def conj_mul(a, b):
    return (a[0] * b[0] + a[1] * b[1], a[0] * b[1] - a[1] * b[0])


def total(pairs):
    return (sum(p[0] for p in pairs[1:]) + pairs[0][0], sum(p[1] for p in pairs[1:]) + pairs[0][1])


def position_terms(fronts, rears, probes, observed, tables, prop):
    length = observed[0].shape[0]
    modes = len(probes)
    ahead, behind = tables
    forward = lambda f: transform(f, ahead, behind, length)
    inverse = lambda f: transform(f, behind, ahead, length)
    each = range(len(fronts) * modes)
    front = lambda i: fronts[i // modes]()
    rear = lambda i: rears[i // modes]()
    probe = lambda i: probes[i % modes]
    spec = forward([mul(probe(i), front(i)) for i in each])
    inner = inverse([mul(s, prop) for s in spec])
    far = forward([mul(inner[i], rear(i)) for i in each])
    resid = []
    for q, seen in enumerate(observed):
        mine = far[q * modes : (q + 1) * modes]
        intensity = sum(re * re + im * im for re, im in mine[1:]) + mine[0][0] ** 2 + mine[0][1] ** 2
        factor = 1.0 - jnp.sqrt(seen) / jnp.sqrt(intensity + 1.0)
        resid += [(re * factor, im * factor) for re, im in mine]
    back_b = inverse(resid)
    back_spec = forward([conj_mul(rear(i), back_b[i]) for i in each])
    back_a = inverse([conj_mul(prop, b) for b in back_spec])
    grads = []
    for q in range(len(fronts)):
        mine = range(q * modes, (q + 1) * modes)
        grads.append(
            (
                total([conj_mul(probe(i), back_a[i]) for i in mine]),
                total([conj_mul(inner[i], back_b[i]) for i in mine]),
            )
        )
    terms = [
        total([conj_mul(fronts[q](), back_a[q * modes + m]) for q in range(len(fronts))])
        for m in range(modes)
    ]
    return grads, terms


def position_kernel(n_tile, n_mode, slots, tile_ref, arrived_ref, probe_ref, meas_ref, table_ref, prop_ref, back_ref, pgrad_ref):
    per_dev = meas_ref.shape[0]
    modes = probe_ref.shape[1]
    owner = lax.axis_index("tile") * n_mode + lax.axis_index("mode")
    tiles, order = ranks(tile_ref, owner * per_dev, per_dev)
    back_ref[...] = jnp.zeros_like(back_ref)
    place = [
        [(tiles[q] * n_mode + k * n_mode // 2) * slots + order[q] for k in range(2)]
        for q in range(per_dev)
    ]

    def window(q, k):
        return lambda: tuple(arrived_ref[place[q][k], part].astype(f32) for part in range(2))

    grads, terms = position_terms(
        [window(q, 0) for q in range(per_dev)],
        [window(q, 1) for q in range(per_dev)],
        [(probe_ref[0, m], probe_ref[1, m]) for m in range(modes)],
        [meas_ref[q] for q in range(per_dev)],
        (table_ref[0], table_ref[1]),
        (prop_ref[0], prop_ref[1]),
    )
    for q in range(per_dev):
        for k in range(2):
            for part in range(2):
                back_ref[place[q][k], part] = grads[q][k][part].astype(bf16)
    for m in range(modes):
        for part in range(2):
            pgrad_ref[part, m] = terms[m][part]


smem = pl.BlockSpec(memory_space=pltpu.SMEM)
vmem = pl.BlockSpec(memory_space=pltpu.VMEM)
params = pltpu.CompilerParams(vmem_limit_bytes=vmem_bytes)


def communicating(number):
    return pltpu.CompilerParams(
        vmem_limit_bytes=vmem_bytes, collective_id=number, has_side_effects=True
    )


def on_device(object_field, probe_modes, measured, pos_tile, off_row, off_col):
    length = probe_modes.shape[-1]
    margin = length // 2
    tile_rows = object_field.shape[2]
    tile_cols = object_field.shape[3]
    per_dev = measured.shape[1]
    n_tile = lax.axis_size("tile")
    n_mode = lax.axis_size("mode")
    slots = max(2, 2 * per_dev // n_tile)
    owners = n_tile * n_mode
    count = owners * slots
    tables, prop = make_tables(length)
    places = (pos_tile[0, :, 0], off_row[0], off_col[0])
    n_strip = lax.axis_size("strip")
    sizes = (per_dev, slots, n_tile, n_mode, n_strip, margin)
    windows = jax.ShapeDtypeStruct((count, 2, length, length), bf16)
    rows, width = tile_rows + 2 * margin, tile_cols + 2 * length
    dma = pltpu.SemaphoreType.DMA
    arrived = pl.pallas_call(
        lambda *refs: forward_kernel(*sizes, *refs),
        out_shape=windows,
        in_specs=[smem] * 3 + [vmem],
        out_specs=vmem,
        scratch_shapes=[
            pltpu.VMEM((2, rows, width), bf16),
            pltpu.VMEM(windows.shape, bf16),
            *[dma((len(directions),))] * 2,
            *[dma((owners,))] * 2,
        ],
        compiler_params=communicating(0),
        name="forward",
    )(*places, object_field[:, 0])
    back, probe_part = pl.pallas_call(
        lambda *refs: position_kernel(n_tile, n_mode, slots, *refs),
        out_shape=(windows, jax.ShapeDtypeStruct(probe_modes.shape, f32)),
        in_specs=[smem] + [vmem] * 5,
        out_specs=(vmem, vmem),
        compiler_params=params,
        name="positions",
    )(places[0], arrived, probe_modes, measured[0], tables, prop)
    flat = probe_part.reshape(-1, length)
    piece = flat.shape[0] // owners
    object_grad, probe_grad = pl.pallas_call(
        lambda *refs: backward_kernel(*sizes, *refs),
        out_shape=(
            jax.ShapeDtypeStruct((2, tile_rows, tile_cols), f32),
            jax.ShapeDtypeStruct(flat.shape, f32),
        ),
        in_specs=[smem] * 3 + [vmem] * 2,
        out_specs=(vmem, vmem),
        scratch_shapes=[
            pltpu.VMEM(windows.shape, bf16),
            pltpu.VMEM((2, rows, width), f32),
            pltpu.VMEM((2, rows, count * length), bf16),
            pltpu.VMEM((count * length, width), bf16),
            pltpu.VMEM((n_mode, n_tile * piece, length), f32),
            pltpu.VMEM((n_tile * piece, length), f32),
            pltpu.VMEM((n_tile, piece, length), f32),
            pltpu.VMEM((piece, length), f32),
            pltpu.VMEM((n_strip, piece, length), f32),
            *[pltpu.VMEM((2, rows, width), bf16)] * 2,
            *[dma((owners,))] * 2,
            *[dma((n_mode,))] * 2,
            *[dma((n_tile,))] * 2,
            *[dma((n_strip,))] * 2,
            *[dma((n_tile,))] * 2,
            *[dma((n_mode,))] * 2,
            *[dma((len(directions),))] * 2,
        ],
        compiler_params=communicating(1),
        name="backward",
    )(*places, back, flat)
    return (object_grad[:, None], probe_grad.reshape(probe_modes.shape))


def solution(mesh):
    return jax.shard_map(
        on_device,
        mesh=mesh,
        in_specs=(
            P("group", "mode", "strip", "tile"),
            P("group", None, None, None),
            P(("group", "strip"), ("tile", "mode"), None, None),
            P(("group", "strip"), None, None),
            P(("group", "strip"), None),
            P(("group", "strip"), None),
        ),
        out_specs=(P("group", "mode", "strip", "tile"), P("group", None, None, None)),
        check_vma=False,
    )
```
